32 devices in a mesh: curve: 4 (over y, x), line: 8 (over z, core).
Axes of the slice: x: 2, y: 2, z: 4, core: 2. Of those that a mesh axis runs over, the one named last changes fastest.
Arguments:
- scaled_distributions: float32 [4, 8, 6, 27, 512], P('curve', 'line'), may hold values from 0.1 to 2.5, as said below
- remaining_brick_places: int32 [4, 8, 6], P('curve', 'line'), may hold values from -1 to 7, as said below
- retained_wavenumbers: int32 [8], replicated, may hold values from 1 to 16, as said below
- regional_amplitudes: float32 [3, 2, 128, 16], P(None, None, 'curve'), may hold values from -0.12 to 0.12
- relaxation_frequencies: float32 [27], replicated, may hold values from 0.6 to 1.8
Outputs:
- new_populations: float32 [4, 8, 6, 27, 512], P('curve', 'line')
The draws below stay inside these ranges and needn't reach their ends.
Inputs may be any that keep to these rules, and one draw needn't show every extreme that they name: `scaled_distributions`: positive values. `remaining_brick_places`: distinct tile positions (row of the block times 4 plus its column) of one device's surviving blocks, -1 in empty slots, which may stand anywhere; at least half of each device's slots are used, and on some device all 6 are. `retained_wavenumbers`: distinct mode numbers; 16 is always among them.
All inputs are finite; a program needn't handle non-finite values.
Results may differ from the reference program's by a relative error of at most 0.0003.
Values sent between devices are 32-bit elements; how exact they have to be, the bound alone decides.
A program may use at most 64 MiB of HBM per device.

```python
import jax
import jax.numpy as jnp
import numpy as np
from jax import lax

BE = 16
LEVELS = 2
TX = 4
TY = 2
KEEP = 8
KMAX = 16
MAX_SEATS_CHIP = 6
GRID_SITES_EACH = 512
NX = 512
NY = 128
N_CURVE = 4
N_LINE = 8


def draw_scaled_distributions(key, part):
    lead_shape = (N_CURVE, N_LINE, MAX_SEATS_CHIP, 1, GRID_SITES_EACH)
    line_place = jnp.arange(N_LINE, dtype=jnp.float32).reshape(1, N_LINE, 1, 1, 1)
    phases = jax.random.uniform(jax.random.fold_in(key, 1), (N_CURVE, 1, 1, 1, 1), jnp.float32, 0.0, 6.2831855)
    wave_angle = 6.2831855 * (line_place + 0.5) / N_LINE + phases
    density_low = 0.9
    density_high = 1.1
    noise_size = 0.25
    wind_x = 0.03 * jnp.sin(wave_angle) + jax.random.uniform(jax.random.fold_in(key, 2), lead_shape, jnp.float32, -0.03, 0.03)
    wind_y = 0.03 * jnp.cos(wave_angle) + jax.random.uniform(jax.random.fold_in(key, 3), lead_shape, jnp.float32, -0.03, 0.03)
    wind_z = jax.random.uniform(jax.random.fold_in(key, 4), lead_shape, jnp.float32, -0.015, 0.015)
    density = jax.random.uniform(jax.random.fold_in(key, 5), lead_shape, jnp.float32, density_low, density_high)
    noise_draw = jax.random.uniform(jax.random.fold_in(key, 6), (N_CURVE, N_LINE, MAX_SEATS_CHIP, 27, GRID_SITES_EACH), jnp.float32, -1.0, 1.0)
    numbers = jnp.arange(27, dtype=jnp.int32)
    speed_x = (numbers // 9 - 1).astype(jnp.float32).reshape(1, 1, 1, 27, 1)
    speed_y = (numbers // 3 % 3 - 1).astype(jnp.float32).reshape(1, 1, 1, 27, 1)
    speed_z = (numbers % 3 - 1).astype(jnp.float32).reshape(1, 1, 1, 27, 1)
    drift = 3.0 * (speed_x * wind_x + speed_y * wind_y + speed_z * wind_z)
    return density * (1.0 + drift + noise_size * noise_draw)


def draw_remaining_brick_places(key, part):
    chip_tally = N_CURVE * N_LINE
    tile_count = TX * TY
    device_keys = jax.random.split(jax.random.fold_in(key, 21), chip_tally)
    tile_sequence = jax.vmap(lambda single: jax.random.permutation(single, tile_count))(device_keys)[:, :MAX_SEATS_CHIP]
    rank_keys = jax.random.split(jax.random.fold_in(key, 22), chip_tally)
    slot_positions = jax.vmap(lambda single: jax.random.permutation(single, MAX_SEATS_CHIP))(rank_keys)
    block_counts = MAX_SEATS_CHIP - jax.random.randint(jax.random.fold_in(key, 23), (chip_tally,), 0, MAX_SEATS_CHIP // 2 + 1)
    fullest = jax.random.randint(jax.random.fold_in(key, 24), (), 0, chip_tally)
    block_counts = jnp.where(jnp.arange(chip_tally) == fullest, MAX_SEATS_CHIP, block_counts)
    kept_block_ids = jnp.where(slot_positions < block_counts[:, None], tile_sequence, -1)
    return kept_block_ids.reshape(N_CURVE, N_LINE, MAX_SEATS_CHIP).astype(jnp.int32)


def draw_retained_wavenumbers(key, part):
    others = jax.random.permutation(jax.random.fold_in(key, 31), KMAX - 1)[:KEEP - 1] + 1
    return jnp.concatenate([jnp.array([KMAX], dtype=jnp.int32), others.astype(jnp.int32)])


def level_of(stream_key, extent, pieces, least, top_value):
    gain, own = 1.0, jax.random.fold_in(stream_key, 6)
    for axis_at, blocks in pieces:
        heights = jnp.exp(jax.random.uniform(jax.random.fold_in(own, axis_at), (blocks,), jnp.float32, least / len(pieces), top_value / len(pieces)))
        gain = gain * jnp.repeat(heights, extent[axis_at] // blocks).reshape([-1 if axis == axis_at else 1 for axis in range(len(extent))])
    return gain


def centred(stream_key, dims, spread, limit, pieces=(), kind=jnp.bfloat16):
    result = jax.random.normal(stream_key, dims, jnp.float32) * spread
    if len(pieces) > 0:
        result = level_of(stream_key, dims, pieces, -0.22, 0.18) * result
    return jnp.clip(result, min=-limit, max=limit).astype(kind)


def setup_inputs(seed: int = 0) -> dict:
    key_list = jax.random.split(jax.random.key(seed), 6)
    return {
        "scaled_distributions": draw_scaled_distributions(jax.random.fold_in(key_list[5], 71), 0),
        "remaining_brick_places": draw_remaining_brick_places(jax.random.fold_in(key_list[5], 71), 0),
        "retained_wavenumbers": draw_retained_wavenumbers(jax.random.fold_in(key_list[5], 71), 0),
        "regional_amplitudes": centred(key_list[3], (3, LEVELS, NY, 2 * KEEP), 0.04, 0.12, ((2, 4),), jnp.float32),
        "relaxation_frequencies": jnp.clip(jax.random.uniform(key_list[4], (27,), jnp.float32, 0.6, 1.8), 0.6, 1.8),
    }


NUDGE_GAIN = 0.5
TWO_PI = 6.283185307179586
HIGHEST = lax.Precision.HIGHEST


def lattice_tables():
    one_weights = np.array([1.0 / 6.0, 2.0 / 3.0, 1.0 / 6.0])
    speeds = np.array([[along_x - 1, along_y - 1, along_z - 1] for along_x in range(3) for along_y in range(3) for along_z in range(3)])
    weights = np.array([one_weights[along_x] * one_weights[along_y] * one_weights[along_z] for along_x in range(3) for along_y in range(3) for along_z in range(3)])
    vander = np.array([[1.0, 1.0, 1.0], [-1.0, 0.0, 1.0], [1.0, 0.0, 1.0]])
    undo_vander = np.array([[0.0, -0.5, 0.5], [1.0, 0.0, -1.0], [0.0, 0.5, 0.5]])
    moment_matrix = np.kron(vander, np.kron(vander, vander))
    inverse = np.kron(undo_vander, np.kron(undo_vander, undo_vander))
    forward = jnp.asarray(moment_matrix * weights[None, :], dtype=jnp.float32)
    backward = jnp.asarray(inverse / weights[:, None], dtype=jnp.float32)
    return forward, backward, speeds


def mode_basis_at(mode_ids, positions, length):
    phase_ids = (positions[:, None] * mode_ids[None, :]) % length
    angles = phase_ids.astype(jnp.float32) * (TWO_PI / length)
    return jnp.concatenate([jnp.cos(angles), jnp.sin(angles)], axis=1)


def cell_moments(device_pops, forward):
    return jnp.einsum('ij,bjc->bic', forward, device_pops, precision=HIGHEST)


def velocity_from(moments):
    return jnp.stack([moments[:, 9], moments[:, 3], moments[:, 1]], axis=1) / moments[:, 0][:, None]


def collide(moments, device_nudge, backward, relaxation_frequencies):
    density = moments[:, 0]
    shifted = velocity_from(moments) + device_nudge
    powers = jnp.stack([jnp.ones_like(shifted), shifted, shifted * shifted + 1.0 / 3.0], axis=1)
    equilibrium = density[:, None, None, None, :] * powers[:, :, None, None, 0] * powers[:, None, :, None, 1] * powers[:, None, None, :, 2]
    equilibrium = equilibrium.reshape(moments.shape)
    relaxed = moments - relaxation_frequencies[None, :, None] * (moments - equilibrium)
    return jnp.einsum('ij,bjc->bic', backward, relaxed, precision=HIGHEST)


def grid_pointers(remaining_brick_places):
    curve_ids = jnp.arange(N_CURVE, dtype=jnp.int32)[:, None, None]
    line_ids = jnp.arange(N_LINE, dtype=jnp.int32)[None, :, None]
    occupied_seats = remaining_brick_places >= 0
    bounded_labels = jnp.maximum(remaining_brick_places, 0)
    row_base = (curve_ids * TY + bounded_labels // TX) * BE
    col_base = (line_ids * TX + bounded_labels % TX) * BE
    within = jnp.arange(BE, dtype=jnp.int32)
    horizontal_label = row_base[..., None, None] + within[:, None]
    vertical_label = col_base[..., None, None] + within[None, :]
    return horizontal_label, vertical_label, occupied_seats


def seats_onto_full(packed_arrangement, remaining_brick_places):
    horizontal_label, vertical_label, occupied_seats = grid_pointers(remaining_brick_places)
    channels = packed_arrangement.shape[3]
    values = packed_arrangement.reshape(N_CURVE, N_LINE, MAX_SEATS_CHIP, channels, LEVELS, BE, BE).transpose(3, 4, 0, 1, 2, 5, 6)
    rows_drop = jnp.where(occupied_seats[..., None, None], horizontal_label, NY + BE)
    full_arrangement = jnp.zeros((channels, LEVELS, NY, NX), packed_arrangement.dtype)
    return full_arrangement.at[:, :, rows_drop, vertical_label].set(values, mode="drop")


def full_onto_seats(full_arrangement, remaining_brick_places):
    horizontal_label, vertical_label, occupied_seats = grid_pointers(remaining_brick_places)
    channels = full_arrangement.shape[0]
    picked = full_arrangement[:, :, horizontal_label, vertical_label]
    picked = picked.transpose(2, 3, 4, 0, 1, 5, 6).reshape(N_CURVE, N_LINE, MAX_SEATS_CHIP, channels, GRID_SITES_EACH)
    return picked * occupied_seats[..., None, None].astype(full_arrangement.dtype)


def reference(scaled_distributions, remaining_brick_places, retained_wavenumbers, regional_amplitudes, relaxation_frequencies):
    forward, backward, speeds = lattice_tables()
    chip_tally = N_CURVE * N_LINE
    flat_pops = scaled_distributions.reshape(chip_tally, MAX_SEATS_CHIP, 27, GRID_SITES_EACH)
    stream_speed_vector = lax.map(lambda device_pops: velocity_from(cell_moments(device_pops, forward)), flat_pops)
    breeze_region = seats_onto_full(stream_speed_vector.reshape(N_CURVE, N_LINE, MAX_SEATS_CHIP, 3, GRID_SITES_EACH), remaining_brick_places)
    mode_basis = mode_basis_at(retained_wavenumbers, jnp.arange(NX, dtype=jnp.int32), NX)
    coefficients = jnp.einsum('klyx,xm->klym', breeze_region, mode_basis, precision=HIGHEST)
    misfit = regional_amplitudes - (2.0 / NX) * coefficients
    forcing_adjustment = NUDGE_GAIN * jnp.einsum('klym,xm->klyx', misfit, mode_basis, precision=HIGHEST)
    forced_sites = full_onto_seats(forcing_adjustment, remaining_brick_places).reshape(chip_tally, MAX_SEATS_CHIP, 3, GRID_SITES_EACH)
    relaxed_populace = lax.map(lambda pair_args: collide(cell_moments(pair_args[0], forward), pair_args[1], backward, relaxation_frequencies), (flat_pops, forced_sites))
    relaxed_populace = relaxed_populace.reshape(N_CURVE, N_LINE, MAX_SEATS_CHIP, 27, GRID_SITES_EACH)
    liquid_region = seats_onto_full(jnp.ones((N_CURVE, N_LINE, MAX_SEATS_CHIP, 1, GRID_SITES_EACH), jnp.float32), remaining_brick_places)[0, 0]
    solid_grid = liquid_region < 0.5
    portion_catalog = []
    for discrete_heading in range(27):
        carry_eastward = int(speeds[discrete_heading, 0])
        carry_northward = int(speeds[discrete_heading, 1])
        step_z = int(speeds[discrete_heading, 2])
        carried_sheet = jnp.roll(seats_onto_full(relaxed_populace[:, :, :, discrete_heading:discrete_heading + 1], remaining_brick_places)[0], (carry_northward, carry_eastward), axis=(1, 2))
        blocked = jnp.roll(solid_grid, (carry_northward, carry_eastward), axis=(0, 1))
        bounced_distributions = seats_onto_full(relaxed_populace[:, :, :, 26 - discrete_heading:27 - discrete_heading], remaining_brick_places)[0]
        if step_z == 0:
            source = carried_sheet
            block_both = jnp.stack([blocked, blocked])
        elif step_z == 1:
            source = jnp.stack([carried_sheet[0], carried_sheet[0]])
            block_both = jnp.stack([jnp.ones_like(blocked), blocked])
        else:
            mirror_sheet = jnp.roll(seats_onto_full(relaxed_populace[:, :, :, discrete_heading + 2:discrete_heading + 3], remaining_brick_places)[0], (carry_northward, carry_eastward), axis=(1, 2))
            source = jnp.stack([carried_sheet[1], mirror_sheet[1]])
            block_both = jnp.stack([blocked, blocked])
        update_outcome = jnp.where(block_both, bounced_distributions, source)
        portion_catalog.append(full_onto_seats(update_outcome[None], remaining_brick_places))
    return jnp.concatenate(portion_catalog, axis=3)
```

```python
import functools

import jax
import jax.numpy as jnp
import numpy as np
from jax import lax
from jax.experimental import pallas as pl
from jax.experimental.pallas import tpu as pltpu
from jax.sharding import PartitionSpec as P

SLOTS = 6
MESH = pl.DeviceIdType.MESH
TWO_PI = 6.283185307179586
HIGHEST = lax.Precision.HIGHEST


def along(items, stride, fn):
    done = list(items)
    for base in range(27):
        if (base // stride) % 3 == 0:
            at = (base, base + stride, base + 2 * stride)
            got = fn(*(items[n] for n in at))
            for n, value in zip(at, got):
                done[n] = value
    return done


def to_moments(low, mid, high):
    both = (low + high) * (1.0 / 6.0)
    return both + mid * (2.0 / 3.0), (high - low) * (1.0 / 6.0), both


def from_moments(m0, m1, m2):
    return (m2 - m1) * 3.0, (m0 - m2) * 1.5, (m1 + m2) * 3.0


def dot(a, b, dims=((1,), (0,))):
    return lax.dot_general(a, b, (dims, ((), ())), precision=HIGHEST,
                           preferred_element_type=jnp.float32)


def lroll(x, shift):
    shift = shift % 128
    return x if shift == 0 else pltpu.roll(x, shift, 1)


def sroll(x, shift):
    return pltpu.roll(x, shift % 8, 0)


def kernel(nc, nl, keys, waves, rates, x_ref, tgt_ref, out_ref,
           g, post, psend, precv, xsend, xrecv, ysend, yrecv, yside,
           ps_sem, pr_sem, xs_sem, xr_sem, ys_sem, yr_sem, ds_sem, dr_sem):
    ci = lax.axis_index("curve")
    li = lax.axis_index("line")

    def line_at(d):
        return lax.rem(li + (d + nl), nl)

    def curve_at(d):
        return lax.rem(ci + (d + nc), nc)

    barrier = pltpu.get_barrier_semaphore()
    friends = [{"curve": ci, "line": line_at(d)} for d in range(1, nl)]
    friends += [{"curve": curve_at(dy), "line": line_at(dx)} for dy in (-1, 1) for dx in (-1, 0, 1)]
    for friend in friends:
        pl.semaphore_signal(barrier, inc=1, device_id=friend, device_id_type=MESH)

    shape = (8, 128)
    lane = lax.broadcasted_iota(jnp.int32, shape, 1)
    sub = lax.broadcasted_iota(jnp.int32, shape, 0)
    q = lane & 15
    chunk = lane >> 4
    tx = sub & 3
    key = [keys[0, 0, s] for s in range(SLOTS)]

    present = sub == key[0]
    for s in range(1, SLOTS):
        present = jnp.logical_or(present, sub == key[s])
    fluid = jnp.where(present, 1.0, 0.0).astype(jnp.float32)
    solid = 1.0 - fluid

    for p in range(8):
        slot = jnp.int32(0)
        for s in range(SLOTS):
            slot = jnp.where(key[s] == p, s, slot)
        for v in range(4):
            g[v, pl.ds(p, 27, stride=8), :] = x_ref[pl.ds(slot * 108 + v, 27, stride=4), :]

    velocity = [[None] * 4 for _ in range(3)]
    for v in range(4):
        f = [g[v, pl.ds(8 * j, 8), :] for j in range(27)]
        for stride in (1, 3, 9):
            f = along(f, stride, to_moments)
        for j in range(27):
            g[v, pl.ds(8 * j, 8), :] = f[j]
        scale = fluid / f[0]
        for k, j in enumerate((9, 3, 1)):
            velocity[k][v] = f[j] * scale

    def wave_lanes(ids):
        m = ids & 7
        out = jnp.full(ids.shape, waves[0], jnp.int32)
        for n in range(1, 8):
            out = jnp.where(m == n, waves[n], out)
        return out

    total_x = nl * 64
    unit = TWO_PI / total_x
    lane16 = lax.broadcasted_iota(jnp.int32, (16, 128), 1)
    row16 = lax.broadcasted_iota(jnp.int32, (16, 128), 0)
    turn = lax.rem(wave_lanes(lane16) * row16, total_x)
    turn = jnp.where((lane16 & 15) >= 8, turn - total_x // 4, turn)
    small = jnp.cos(turn.astype(jnp.float32) * unit)
    rowb = lax.broadcasted_iota(jnp.int32, (128, 128), 0)
    laneb = lax.broadcasted_iota(jnp.int32, (128, 128), 1)
    basis = jnp.where((rowb >> 4) == (laneb >> 4), jnp.concatenate([small] * 8, axis=0), 0.0)

    start = lax.rem(wave_lanes(lane) * ((li * 4 + tx) * 16), total_x)
    angle = start.astype(jnp.float32) * unit
    cos0 = jnp.cos(angle)
    sin0 = jnp.cos((start - total_x // 4).astype(jnp.float32) * unit)
    is_sin = q >= 8
    sin_signed = jnp.where(is_sin, sin0, -sin0)
    cos96 = jnp.concatenate([cos0] * 12, axis=0)
    sin96 = jnp.concatenate([sin_signed] * 12, axis=0)
    is_sin96 = (lax.broadcasted_iota(jnp.int32, (96, 128), 1) & 15) >= 8

    def swapped(t):
        return jnp.where(is_sin96, pltpu.roll(t, 8, 1), pltpu.roll(t, 120, 1))

    r24 = lax.broadcasted_iota(jnp.int32, (24, 96), 0)
    c96 = lax.broadcasted_iota(jnp.int32, (24, 96), 1)
    same = (r24 >> 2) == (c96 >> 4)
    same = jnp.logical_and(same, ((r24 >> 1) & 1) == ((c96 >> 2) & 1))
    same = jnp.logical_and(same, (r24 & 1) == ((c96 >> 3) & 1))
    gather = jnp.where(same, 1.0, 0.0).astype(jnp.float32)

    stack = jnp.concatenate([velocity[k][v] for k in range(3) for v in range(4)], axis=0)
    local = dot(stack, basis)
    local = local * cos96 + swapped(local) * sin96
    psend[...] = dot(gather, local)

    pl.semaphore_wait(barrier, len(friends))

    copies = []
    for d in range(1, nl):
        copy = pltpu.make_async_remote_copy(
            src_ref=psend, dst_ref=precv.at[d - 1], send_sem=ps_sem.at[d - 1],
            recv_sem=pr_sem.at[d - 1], device_id={"curve": ci, "line": line_at(d)},
            device_id_type=MESH)
        copy.start()
        copies.append(copy)
    ry = lax.broadcasted_iota(jnp.int32, (32, 512), 0)
    ly = lax.broadcasted_iota(jnp.int32, (32, 512), 1)
    spread = dot(tgt_ref[...], jnp.where((ly >> 4) == ry, 1.0, 0.0).astype(jnp.float32))
    rm = lax.broadcasted_iota(jnp.int32, (96, 512), 0)
    lm = lax.broadcasted_iota(jnp.int32, (96, 512), 1)
    spread = jnp.where((rm & 15) == (lm & 15), spread, 0.0)
    target = jnp.zeros((24, 128), jnp.float32)
    for yy in range(4):
        pick = jnp.logical_and((r24 >> 2) == (c96 >> 4), (r24 & 3) == yy)
        target = target + dot(jnp.where(pick, 1.0, 0.0).astype(jnp.float32),
                              spread[:, 128 * yy:128 * yy + 128])

    total = psend[...]
    for d in range(1, nl):
        copies[d - 1].wait_recv()
        total = total + precv[d - 1]
    for copy in copies:
        copy.wait_send()

    misfit = 0.5 * (target - (2.0 / total_x) * total)
    wide = dot(gather, misfit, ((0,), (0,)))
    wide = wide * cos96 - swapped(wide) * sin96
    nudge = dot(wide, basis, ((1,), (1,)))

    for v in range(4):
        m = [g[v, pl.ds(8 * j, 8), :] for j in range(27)]
        powers = []
        for k in range(3):
            at = 8 * (4 * k + v)
            shifted = velocity[k][v] + nudge[at:at + 8, :]
            powers.append((None, shifted, shifted * shifted + 1.0 / 3.0))
        relaxed = []
        for a in range(3):
            along_a = m[0] if a == 0 else m[0] * powers[0][a]
            for b in range(3):
                along_b = along_a if b == 0 else along_a * powers[1][b]
                for c in range(3):
                    eq = along_b if c == 0 else along_b * powers[2][c]
                    j = 9 * a + 3 * b + c
                    relaxed.append(m[j] - rates[j] * (m[j] - eq))
        for stride in (1, 3, 9):
            relaxed = along(relaxed, stride, from_moments)
        for j in range(27):
            post[v, pl.ds(8 * j, 8), :] = relaxed[j]

    def at(j, v):
        return post[v, pl.ds(8 * j, 8), :]

    for n, cx in enumerate((1, -1)):
        for v in range(4):
            pack = solid
            for k in range(9):
                moved = lroll(at(9 * (cx + 1) + k, v), k - 15 if cx == 1 else k)
                pack = jnp.where(q == k, moved, pack)
            xsend[n, v] = pack
    for n, cy in enumerate((1, -1)):
        for cx in (-1, 0, 1):
            pack = solid
            for cz in range(3):
                for z in range(2):
                    c = 2 * cz + z
                    j = 9 * (cx + 1) + 3 * (cy + 1) + cz
                    if cy == 1:
                        moved = lroll(at(j, 2 * z + 1), 16 * c - 112)
                    else:
                        moved = lroll(at(j, 2 * z), 16 * c)
                    pack = jnp.where(chunk == c, moved, pack)
            ysend[n, cx + 1] = pack

    halo = []
    for n, cy in enumerate((1, -1)):
        halo.append(pltpu.make_async_remote_copy(
            src_ref=ysend.at[n], dst_ref=yrecv.at[n], send_sem=ys_sem.at[n],
            recv_sem=yr_sem.at[n], device_id={"curve": curve_at(cy), "line": li},
            device_id_type=MESH))
        for e, cx in enumerate((1, -1)):
            halo.append(pltpu.make_async_remote_copy(
                src_ref=ysend.at[n, cx + 1], dst_ref=yside.at[n, e],
                send_sem=ds_sem.at[n, e], recv_sem=dr_sem.at[n, e],
                device_id={"curve": curve_at(cy), "line": line_at(cx)},
                device_id_type=MESH))
    for n, cx in enumerate((1, -1)):
        halo.append(pltpu.make_async_remote_copy(
            src_ref=xsend.at[n], dst_ref=xrecv.at[n], send_sem=xs_sem.at[n],
            recv_sem=xr_sem.at[n], device_id={"curve": ci, "line": line_at(cx)},
            device_id_type=MESH))
    for copy in halo:
        copy.start()
    for copy in halo:
        copy.wait()

    def beside(own, other, cx):
        if cx == 1:
            return jnp.where(tx == 0, sroll(other, 5), sroll(own, 1))
        return jnp.where(tx == 3, sroll(other, 3), sroll(own, 7))

    def x_edge(cx):
        return q == (0 if cx == 1 else 15)

    rows_in = {}
    for n, cy in enumerate((1, -1)):
        for cx in (-1, 0, 1):
            row = yrecv[n, cx + 1]
            if cx != 0:
                near = beside(row, yside[n, 0 if cx == 1 else 1], cx)
                row = jnp.where(x_edge(cx), lroll(near, -15 * cx), lroll(row, cx))
            rows_in[cx, cy] = sroll(row, 4)
    cols_in = {}
    for n, cx in enumerate((1, -1)):
        for v in range(4):
            cols_in[cx, v] = beside(xsend[n, v], xrecv[n, v], cx)

    def step_x(own, cx, k, v):
        if cx == 0:
            return own
        near = lroll(cols_in[cx, v], -k if cx == 1 else 15 - k)
        return jnp.where(x_edge(cx), near, lroll(own, cx))

    def step_y(a0, a1, cx, cy, c):
        if cy == 0:
            return a0, a1
        r0, r1 = lroll(a0, 16 * cy), lroll(a1, 16 * cy)
        if cy == 1:
            row = lroll(rows_in[cx, cy], -16 * c)
            row = jnp.where(sub < 4, row, sroll(r1, 4))
            return jnp.where(lane < 16, row, r0), jnp.where(lane < 16, r0, r1)
        row = lroll(rows_in[cx, cy], 112 - 16 * c)
        row = jnp.where(sub >= 4, row, sroll(r0, 4))
        return jnp.where(lane >= 112, r1, r0), jnp.where(lane >= 112, row, r1)

    for cx in (-1, 0, 1):
        for cy in (-1, 0, 1):
            base = 9 * (cx + 1) + 3 * (cy + 1)
            if cx == 0 and cy == 0:
                blocked = None
            else:
                wall = step_x(solid, cx, 9, 0)
                walls = step_y(wall, wall, cx, cy, 6)
                blocked = [w > 0.5 for w in walls]

            def moved(cz, z):
                j = base + cz
                k = 3 * (cy + 1) + cz
                a = [step_x(at(j, 2 * z + h), cx, k, 2 * z + h) for h in range(2)]
                return step_y(a[0], a[1], cx, cy, 2 * cz + z)

            def put(cz, z, source):
                j = base + cz
                for h in range(2):
                    value = at(26 - j, 2 * z + h)
                    if source is not None:
                        value = source[h] if blocked is None else jnp.where(blocked[h], value, source[h])
                    g[2 * z + h, pl.ds(8 * j, 8), :] = value

            put(1, 0, moved(1, 0))
            put(1, 1, moved(1, 1))
            put(2, 0, None)
            put(2, 1, moved(2, 0))
            put(0, 0, moved(0, 1))
            put(0, 1, moved(2, 1))

    for s in range(SLOTS):
        place = jnp.maximum(key[s], 0)
        keep = jnp.where(key[s] >= 0, 1.0, 0.0).astype(jnp.float32)
        for v in range(4):
            out_ref[pl.ds(108 * s + v, 27, stride=4), :] = g[v, pl.ds(place, 27, stride=8), :] * keep


def solution(mesh):
    nc, nl = mesh.shape["curve"], mesh.shape["line"]

    def on_device(scaled, places, waves, amplitudes, rates):
        x = scaled.reshape(SLOTS * 108, 128)
        target = amplitudes.transpose(0, 1, 3, 2).reshape(96, 32)
        vmem = pl.BlockSpec(memory_space=pltpu.VMEM)
        smem = pl.BlockSpec(memory_space=pltpu.SMEM)
        f32 = jnp.float32
        dma = pltpu.SemaphoreType.DMA
        out = pl.pallas_call(
            functools.partial(kernel, nc, nl),
            out_shape=jax.ShapeDtypeStruct((SLOTS * 108, 128), f32),
            in_specs=[smem, smem, smem, vmem, vmem],
            out_specs=vmem,
            scratch_shapes=[
                pltpu.VMEM((4, 216, 128), f32),
                pltpu.VMEM((4, 216, 128), f32),
                pltpu.VMEM((24, 128), f32),
                pltpu.VMEM((nl - 1, 24, 128), f32),
                pltpu.VMEM((2, 4, 8, 128), f32),
                pltpu.VMEM((2, 4, 8, 128), f32),
                pltpu.VMEM((2, 3, 8, 128), f32),
                pltpu.VMEM((2, 3, 8, 128), f32),
                pltpu.VMEM((2, 2, 8, 128), f32),
                dma((nl - 1,)), dma((nl - 1,)),
                dma((2,)), dma((2,)), dma((2,)), dma((2,)),
                dma((2, 2)), dma((2, 2)),
            ],
            compiler_params=pltpu.CompilerParams(collective_id=0, has_side_effects=True),
        )(places, waves, rates, x, target)
        return out.reshape(1, 1, SLOTS, 27, 512)

    return jax.shard_map(
        on_device,
        mesh=mesh,
        in_specs=(
            P("curve", "line", None, None, None),
            P("curve", "line", None),
            P(),
            P(None, None, "curve", None),
            P(),
        ),
        out_specs=P("curve", "line", None, None, None),
        check_vma=False,
    )
```

```python
import functools

import jax
import jax.numpy as jnp
import numpy as np
from jax import lax
from jax.experimental import pallas as pl
from jax.experimental.pallas import tpu as pltpu
from jax.sharding import PartitionSpec as P

SLOTS = 6
MESH = pl.DeviceIdType.MESH
TWO_PI = 6.283185307179586
HIGHEST = lax.Precision.HIGHEST


def along(items, stride, fn):
    done = list(items)
    for base in range(27):
        if (base // stride) % 3 == 0:
            at = (base, base + stride, base + 2 * stride)
            got = fn(*(items[n] for n in at))
            for n, value in zip(at, got):
                done[n] = value
    return done


def to_moments(low, mid, high):
    both = (low + high) * (1.0 / 6.0)
    return both + mid * (2.0 / 3.0), (high - low) * (1.0 / 6.0), both


def from_moments(m0, m1, m2):
    return (m2 - m1) * 3.0, (m0 - m2) * 1.5, (m1 + m2) * 3.0


def dot(a, b, dims=((1,), (0,))):
    return lax.dot_general(a, b, (dims, ((), ())), precision=HIGHEST,
                           preferred_element_type=jnp.float32)


def lroll(x, shift):
    shift = shift % 128
    return x if shift == 0 else pltpu.roll(x, shift, 1)


def sroll(x, shift):
    return pltpu.roll(x, shift % 8, 0)


def collide(nc, nl, keys, waves, rates, x_ref, tgt_ref, post, cols_ref, rows_ref,
           g, psend, precv, xsend, xrecv, ysend, yrecv, yside,
           ps_sem, pr_sem, xs_sem, xr_sem, ys_sem, yr_sem, ds_sem, dr_sem):
    ci = lax.axis_index("curve")
    li = lax.axis_index("line")

    def line_at(d):
        return lax.rem(li + (d + nl), nl)

    def curve_at(d):
        return lax.rem(ci + (d + nc), nc)

    barrier = pltpu.get_barrier_semaphore()
    friends = [{"curve": ci, "line": line_at(d)} for d in range(1, nl)]
    friends += [{"curve": curve_at(dy), "line": line_at(dx)} for dy in (-1, 1) for dx in (-1, 0, 1)]
    for friend in friends:
        pl.semaphore_signal(barrier, inc=1, device_id=friend, device_id_type=MESH)

    shape = (8, 128)
    lane = lax.broadcasted_iota(jnp.int32, shape, 1)
    sub = lax.broadcasted_iota(jnp.int32, shape, 0)
    q = lane & 15
    chunk = lane >> 4
    tx = sub & 3
    key = [keys[0, 0, s] for s in range(SLOTS)]

    present = sub == key[0]
    for s in range(1, SLOTS):
        present = jnp.logical_or(present, sub == key[s])
    fluid = jnp.where(present, 1.0, 0.0).astype(jnp.float32)
    solid = 1.0 - fluid

    for p in range(8):
        slot = jnp.int32(0)
        for s in range(SLOTS):
            slot = jnp.where(key[s] == p, s, slot)
        for v in range(4):
            g[v, pl.ds(p, 27, stride=8), :] = x_ref[pl.ds(slot * 108 + v, 27, stride=4), :]

    velocity = [[None] * 4 for _ in range(3)]
    for v in range(4):
        f = [g[v, pl.ds(8 * j, 8), :] for j in range(27)]
        for stride in (1, 3, 9):
            f = along(f, stride, to_moments)
        for j in range(27):
            g[v, pl.ds(8 * j, 8), :] = f[j]
        scale = fluid / f[0]
        for k, j in enumerate((9, 3, 1)):
            velocity[k][v] = f[j] * scale

    def wave_lanes(ids):
        m = ids & 7
        out = jnp.full(ids.shape, waves[0], jnp.int32)
        for n in range(1, 8):
            out = jnp.where(m == n, waves[n], out)
        return out

    total_x = nl * 64
    unit = TWO_PI / total_x
    lane16 = lax.broadcasted_iota(jnp.int32, (16, 128), 1)
    row16 = lax.broadcasted_iota(jnp.int32, (16, 128), 0)
    turn = lax.rem(wave_lanes(lane16) * row16, total_x)
    turn = jnp.where((lane16 & 15) >= 8, turn - total_x // 4, turn)
    small = jnp.cos(turn.astype(jnp.float32) * unit)
    rowb = lax.broadcasted_iota(jnp.int32, (128, 128), 0)
    laneb = lax.broadcasted_iota(jnp.int32, (128, 128), 1)
    basis = jnp.where((rowb >> 4) == (laneb >> 4), jnp.concatenate([small] * 8, axis=0), 0.0)

    start = lax.rem(wave_lanes(lane) * ((li * 4 + tx) * 16), total_x)
    angle = start.astype(jnp.float32) * unit
    cos0 = jnp.cos(angle)
    sin0 = jnp.cos((start - total_x // 4).astype(jnp.float32) * unit)
    is_sin = q >= 8
    sin_signed = jnp.where(is_sin, sin0, -sin0)
    cos96 = jnp.concatenate([cos0] * 12, axis=0)
    sin96 = jnp.concatenate([sin_signed] * 12, axis=0)
    is_sin96 = (lax.broadcasted_iota(jnp.int32, (96, 128), 1) & 15) >= 8

    def swapped(t):
        return jnp.where(is_sin96, pltpu.roll(t, 8, 1), pltpu.roll(t, 120, 1))

    r24 = lax.broadcasted_iota(jnp.int32, (24, 96), 0)
    c96 = lax.broadcasted_iota(jnp.int32, (24, 96), 1)
    same = (r24 >> 2) == (c96 >> 4)
    same = jnp.logical_and(same, ((r24 >> 1) & 1) == ((c96 >> 2) & 1))
    same = jnp.logical_and(same, (r24 & 1) == ((c96 >> 3) & 1))
    gather = jnp.where(same, 1.0, 0.0).astype(jnp.float32)

    stack = jnp.concatenate([velocity[k][v] for k in range(3) for v in range(4)], axis=0)
    local = dot(stack, basis)
    local = local * cos96 + swapped(local) * sin96
    psend[...] = dot(gather, local)

    pl.semaphore_wait(barrier, len(friends))

    copies = []
    for d in range(1, nl):
        copy = pltpu.make_async_remote_copy(
            src_ref=psend, dst_ref=precv.at[d - 1], send_sem=ps_sem.at[d - 1],
            recv_sem=pr_sem.at[d - 1], device_id={"curve": ci, "line": line_at(d)},
            device_id_type=MESH)
        copy.start()
        copies.append(copy)
    ry = lax.broadcasted_iota(jnp.int32, (32, 512), 0)
    ly = lax.broadcasted_iota(jnp.int32, (32, 512), 1)
    spread = dot(tgt_ref[...], jnp.where((ly >> 4) == ry, 1.0, 0.0).astype(jnp.float32))
    rm = lax.broadcasted_iota(jnp.int32, (96, 512), 0)
    lm = lax.broadcasted_iota(jnp.int32, (96, 512), 1)
    spread = jnp.where((rm & 15) == (lm & 15), spread, 0.0)
    target = jnp.zeros((24, 128), jnp.float32)
    for yy in range(4):
        pick = jnp.logical_and((r24 >> 2) == (c96 >> 4), (r24 & 3) == yy)
        target = target + dot(jnp.where(pick, 1.0, 0.0).astype(jnp.float32),
                              spread[:, 128 * yy:128 * yy + 128])

    total = psend[...]
    for d in range(1, nl):
        copies[d - 1].wait_recv()
        total = total + precv[d - 1]
    for copy in copies:
        copy.wait_send()

    misfit = 0.5 * (target - (2.0 / total_x) * total)
    wide = dot(gather, misfit, ((0,), (0,)))
    wide = wide * cos96 - swapped(wide) * sin96
    nudge = dot(wide, basis, ((1,), (1,)))

    for v in range(4):
        m = [g[v, pl.ds(8 * j, 8), :] for j in range(27)]
        powers = []
        for k in range(3):
            at = 8 * (4 * k + v)
            shifted = velocity[k][v] + nudge[at:at + 8, :]
            powers.append((None, shifted, shifted * shifted + 1.0 / 3.0))
        relaxed = []
        for a in range(3):
            along_a = m[0] if a == 0 else m[0] * powers[0][a]
            for b in range(3):
                along_b = along_a if b == 0 else along_a * powers[1][b]
                for c in range(3):
                    eq = along_b if c == 0 else along_b * powers[2][c]
                    j = 9 * a + 3 * b + c
                    relaxed.append(m[j] - rates[j] * (m[j] - eq))
        for stride in (1, 3, 9):
            relaxed = along(relaxed, stride, from_moments)
        for j in range(27):
            post[v, pl.ds(8 * j, 8), :] = relaxed[j]

    def at(j, v):
        return post[v, pl.ds(8 * j, 8), :]

    halo = []
    for n, cy in enumerate((1, -1)):
        for cx in (-1, 0, 1):
            pack = solid
            for cz in range(3):
                for z in range(2):
                    c = 2 * cz + z
                    j = 9 * (cx + 1) + 3 * (cy + 1) + cz
                    if cy == 1:
                        moved = lroll(at(j, 2 * z + 1), 16 * c - 112)
                    else:
                        moved = lroll(at(j, 2 * z), 16 * c)
                    pack = jnp.where(chunk == c, moved, pack)
            ysend[n, cx + 1] = pack
        for e, cx in enumerate((1, -1)):
            halo.append(pltpu.make_async_remote_copy(
                src_ref=ysend.at[n, cx + 1], dst_ref=yside.at[n, e],
                send_sem=ds_sem.at[n, e], recv_sem=dr_sem.at[n, e],
                device_id={"curve": curve_at(cy), "line": line_at(cx)},
                device_id_type=MESH))
            halo[-1].start()
        halo.append(pltpu.make_async_remote_copy(
            src_ref=ysend.at[n], dst_ref=yrecv.at[n], send_sem=ys_sem.at[n],
            recv_sem=yr_sem.at[n], device_id={"curve": curve_at(cy), "line": li},
            device_id_type=MESH))
        halo[-1].start()
    for n, cx in enumerate((1, -1)):
        for v in range(4):
            pack = solid
            for k in range(9):
                moved = lroll(at(9 * (cx + 1) + k, v), k - 15 if cx == 1 else k)
                pack = jnp.where(q == k, moved, pack)
            xsend[n, v] = pack
        halo.append(pltpu.make_async_remote_copy(
            src_ref=xsend.at[n], dst_ref=xrecv.at[n], send_sem=xs_sem.at[n],
            recv_sem=xr_sem.at[n], device_id={"curve": ci, "line": line_at(cx)},
            device_id_type=MESH))
        halo[-1].start()
    for copy in halo:
        copy.wait()

    def beside(own, other, cx):
        if cx == 1:
            return jnp.where(tx == 0, sroll(other, 5), sroll(own, 1))
        return jnp.where(tx == 3, sroll(other, 3), sroll(own, 7))

    def x_edge(cx):
        return q == (0 if cx == 1 else 15)

    for n, cy in enumerate((1, -1)):
        for cx in (-1, 0, 1):
            row = yrecv[n, cx + 1]
            if cx != 0:
                near = beside(row, yside[n, 0 if cx == 1 else 1], cx)
                row = jnp.where(x_edge(cx), lroll(near, -15 * cx), lroll(row, cx))
            rows_ref[n, cx + 1] = sroll(row, 4)
    for n, cx in enumerate((1, -1)):
        for v in range(4):
            cols_ref[n, v] = beside(xsend[n, v], xrecv[n, v], cx)


def stream(keys, post, cols_ref, rows_ref, out_ref, g):
    shape = (8, 128)
    lane = lax.broadcasted_iota(jnp.int32, shape, 1)
    sub = lax.broadcasted_iota(jnp.int32, shape, 0)
    q = lane & 15
    key = [keys[0, 0, s] for s in range(SLOTS)]

    present = sub == key[0]
    for s in range(1, SLOTS):
        present = jnp.logical_or(present, sub == key[s])
    solid = jnp.where(present, 0.0, 1.0).astype(jnp.float32)

    def at(j, v):
        return post[v, pl.ds(8 * j, 8), :]

    def x_edge(cx):
        return q == (0 if cx == 1 else 15)

    def step_x(own, cx, k, v):
        if cx == 0:
            return own
        near = lroll(cols_ref[0 if cx == 1 else 1, v], -k if cx == 1 else 15 - k)
        return jnp.where(x_edge(cx), near, lroll(own, cx))

    def step_y(a0, a1, cx, cy, c):
        if cy == 0:
            return a0, a1
        r0, r1 = lroll(a0, 16 * cy), lroll(a1, 16 * cy)
        if cy == 1:
            row = lroll(rows_ref[0 if cy == 1 else 1, cx + 1], -16 * c)
            row = jnp.where(sub < 4, row, sroll(r1, 4))
            return jnp.where(lane < 16, row, r0), jnp.where(lane < 16, r0, r1)
        row = lroll(rows_ref[0 if cy == 1 else 1, cx + 1], 112 - 16 * c)
        row = jnp.where(sub >= 4, row, sroll(r0, 4))
        return jnp.where(lane >= 112, r1, r0), jnp.where(lane >= 112, row, r1)

    for cx in (-1, 0, 1):
        for cy in (-1, 0, 1):
            base = 9 * (cx + 1) + 3 * (cy + 1)
            if cx == 0 and cy == 0:
                blocked = None
            else:
                wall = step_x(solid, cx, 9, 0)
                walls = step_y(wall, wall, cx, cy, 6)
                blocked = [w > 0.5 for w in walls]

            def moved(cz, z):
                j = base + cz
                k = 3 * (cy + 1) + cz
                a = [step_x(at(j, 2 * z + h), cx, k, 2 * z + h) for h in range(2)]
                return step_y(a[0], a[1], cx, cy, 2 * cz + z)

            def put(cz, z, source):
                j = base + cz
                for h in range(2):
                    value = at(26 - j, 2 * z + h)
                    if source is not None:
                        value = source[h] if blocked is None else jnp.where(blocked[h], value, source[h])
                    g[2 * z + h, pl.ds(8 * j, 8), :] = value

            put(1, 0, moved(1, 0))
            put(1, 1, moved(1, 1))
            put(2, 0, None)
            put(2, 1, moved(2, 0))
            put(0, 0, moved(0, 1))
            put(0, 1, moved(2, 1))

    for s in range(SLOTS):
        place = jnp.maximum(key[s], 0)
        keep = jnp.where(key[s] >= 0, 1.0, 0.0).astype(jnp.float32)
        for v in range(4):
            out_ref[pl.ds(108 * s + v, 27, stride=4), :] = g[v, pl.ds(place, 27, stride=8), :] * keep


def solution(mesh):
    nc, nl = mesh.shape["curve"], mesh.shape["line"]

    def on_device(scaled, places, waves, amplitudes, rates):
        x = scaled.reshape(SLOTS * 108, 128)
        target = amplitudes.transpose(0, 1, 3, 2).reshape(96, 32)
        vmem = pl.BlockSpec(memory_space=pltpu.VMEM)
        smem = pl.BlockSpec(memory_space=pltpu.SMEM)
        f32 = jnp.float32
        dma = pltpu.SemaphoreType.DMA
        post, cols, rows = pl.pallas_call(
            functools.partial(collide, nc, nl),
            out_shape=[
                jax.ShapeDtypeStruct((4, 216, 128), f32),
                jax.ShapeDtypeStruct((2, 4, 8, 128), f32),
                jax.ShapeDtypeStruct((2, 3, 8, 128), f32),
            ],
            in_specs=[smem, smem, smem, vmem, vmem],
            out_specs=[vmem] * 3,
            scratch_shapes=[
                pltpu.VMEM((4, 216, 128), f32),
                pltpu.VMEM((24, 128), f32),
                pltpu.VMEM((nl - 1, 24, 128), f32),
                pltpu.VMEM((2, 4, 8, 128), f32),
                pltpu.VMEM((2, 4, 8, 128), f32),
                pltpu.VMEM((2, 3, 8, 128), f32),
                pltpu.VMEM((2, 3, 8, 128), f32),
                pltpu.VMEM((2, 2, 8, 128), f32),
                dma((nl - 1,)), dma((nl - 1,)),
                dma((2,)), dma((2,)), dma((2,)), dma((2,)),
                dma((2, 2)), dma((2, 2)),
            ],
            compiler_params=pltpu.CompilerParams(collective_id=0, has_side_effects=True),
        )(places, waves, rates, x, target)
        out = pl.pallas_call(
            stream,
            out_shape=jax.ShapeDtypeStruct((SLOTS * 108, 128), f32),
            in_specs=[smem, vmem, vmem, vmem],
            out_specs=vmem,
            scratch_shapes=[pltpu.VMEM((4, 216, 128), f32)],
        )(places, post, cols, rows)
        return out.reshape(1, 1, SLOTS, 27, 512)

    return jax.shard_map(
        on_device,
        mesh=mesh,
        in_specs=(
            P("curve", "line", None, None, None),
            P("curve", "line", None),
            P(),
            P(None, None, "curve", None),
            P(),
        ),
        out_specs=P("curve", "line", None, None, None),
        check_vma=False,
    )
```

```python
import functools

import jax
import jax.numpy as jnp
import numpy as np
from jax import lax
from jax.experimental import pallas as pl
from jax.experimental.pallas import tpu as pltpu
from jax.sharding import PartitionSpec as P

SLOTS = 6
MESH = pl.DeviceIdType.MESH
TWO_PI = 6.283185307179586
HIGHEST = lax.Precision.HIGHEST


def along(items, stride, fn):
    done = list(items)
    for base in range(27):
        if (base // stride) % 3 == 0:
            at = (base, base + stride, base + 2 * stride)
            got = fn(*(items[n] for n in at))
            for n, value in zip(at, got):
                done[n] = value
    return done


def to_moments(low, mid, high):
    both = (low + high) * (1.0 / 6.0)
    return both + mid * (2.0 / 3.0), (high - low) * (1.0 / 6.0), both


def from_moments(m0, m1, m2):
    return (m2 - m1) * 3.0, (m0 - m2) * 1.5, (m1 + m2) * 3.0


def dot(a, b, dims=((1,), (0,))):
    return lax.dot_general(a, b, (dims, ((), ())), precision=HIGHEST,
                           preferred_element_type=jnp.float32)


def lroll(x, shift):
    shift = shift % 128
    return x if shift == 0 else pltpu.roll(x, shift, 1)


def sroll(x, shift):
    return pltpu.roll(x, shift % 8, 0)


def collide(nc, nl, keys, waves, rates, x_in, tgt_in, post_out, cols_ref, rows_ref,
            x_ref, tgt_ref, post, g, psend, precv, xsend, xrecv, ysend, yrecv, yside,
           ps_sem, pr_sem, xs_sem, xr_sem, ys_sem, yr_sem, ds_sem, dr_sem, io_sem):
    ci = lax.axis_index("curve")
    li = lax.axis_index("line")

    fetch = pltpu.make_async_copy(x_in, x_ref, io_sem.at[0])
    fetch.start()
    fetch_target = pltpu.make_async_copy(tgt_in, tgt_ref, io_sem.at[1])
    fetch_target.start()

    def line_at(d):
        return lax.rem(li + (d + nl), nl)

    def curve_at(d):
        return lax.rem(ci + (d + nc), nc)

    barrier = pltpu.get_barrier_semaphore()
    friends = [{"curve": ci, "line": line_at(d)} for d in range(1, nl)]
    friends += [{"curve": curve_at(dy), "line": line_at(dx)} for dy in (-1, 1) for dx in (-1, 0, 1)]
    for friend in friends:
        pl.semaphore_signal(barrier, inc=1, device_id=friend, device_id_type=MESH)

    shape = (8, 128)
    lane = lax.broadcasted_iota(jnp.int32, shape, 1)
    sub = lax.broadcasted_iota(jnp.int32, shape, 0)
    q = lane & 15
    chunk = lane >> 4
    tx = sub & 3
    key = [keys[0, 0, s] for s in range(SLOTS)]

    present = sub == key[0]
    for s in range(1, SLOTS):
        present = jnp.logical_or(present, sub == key[s])
    fluid = jnp.where(present, 1.0, 0.0).astype(jnp.float32)
    solid = 1.0 - fluid

    def wave_lanes(ids):
        m = ids & 7
        out = jnp.full(ids.shape, waves[0], jnp.int32)
        for n in range(1, 8):
            out = jnp.where(m == n, waves[n], out)
        return out

    total_x = nl * 64
    unit = TWO_PI / total_x
    lane16 = lax.broadcasted_iota(jnp.int32, (16, 128), 1)
    row16 = lax.broadcasted_iota(jnp.int32, (16, 128), 0)
    turn = lax.rem(wave_lanes(lane16) * row16, total_x)
    turn = jnp.where((lane16 & 15) >= 8, turn - total_x // 4, turn)
    small = jnp.cos(turn.astype(jnp.float32) * unit)
    rowb = lax.broadcasted_iota(jnp.int32, (128, 128), 0)
    laneb = lax.broadcasted_iota(jnp.int32, (128, 128), 1)
    basis = jnp.where((rowb >> 4) == (laneb >> 4), jnp.concatenate([small] * 8, axis=0), 0.0)

    start = lax.rem(wave_lanes(lane) * ((li * 4 + tx) * 16), total_x)
    angle = start.astype(jnp.float32) * unit
    cos0 = jnp.cos(angle)
    sin0 = jnp.cos((start - total_x // 4).astype(jnp.float32) * unit)
    is_sin = q >= 8
    sin_signed = jnp.where(is_sin, sin0, -sin0)
    cos96 = jnp.concatenate([cos0] * 12, axis=0)
    sin96 = jnp.concatenate([sin_signed] * 12, axis=0)
    is_sin96 = (lax.broadcasted_iota(jnp.int32, (96, 128), 1) & 15) >= 8

    def swapped(t):
        return jnp.where(is_sin96, pltpu.roll(t, 8, 1), pltpu.roll(t, 120, 1))

    r24 = lax.broadcasted_iota(jnp.int32, (24, 96), 0)
    c96 = lax.broadcasted_iota(jnp.int32, (24, 96), 1)
    same = (r24 >> 2) == (c96 >> 4)
    same = jnp.logical_and(same, ((r24 >> 1) & 1) == ((c96 >> 2) & 1))
    same = jnp.logical_and(same, (r24 & 1) == ((c96 >> 3) & 1))
    gather = jnp.where(same, 1.0, 0.0).astype(jnp.float32)

    fetch.wait()
    for p in range(8):
        slot = jnp.int32(0)
        for s in range(SLOTS):
            slot = jnp.where(key[s] == p, s, slot)
        for v in range(4):
            g[v, pl.ds(p, 27, stride=8), :] = x_ref[pl.ds(slot * 108 + v, 27, stride=4), :]

    velocity = [[None] * 4 for _ in range(3)]
    for v in range(4):
        f = [g[v, pl.ds(8 * j, 8), :] for j in range(27)]
        for stride in (1, 3, 9):
            f = along(f, stride, to_moments)
        for j in range(27):
            g[v, pl.ds(8 * j, 8), :] = f[j]
        scale = fluid / f[0]
        for k, j in enumerate((9, 3, 1)):
            velocity[k][v] = f[j] * scale

    stack = jnp.concatenate([velocity[k][v] for k in range(3) for v in range(4)], axis=0)
    local = dot(stack, basis)
    local = local * cos96 + swapped(local) * sin96
    psend[...] = dot(gather, local)

    pl.semaphore_wait(barrier, len(friends))

    copies = []
    for d in range(1, nl):
        copy = pltpu.make_async_remote_copy(
            src_ref=psend, dst_ref=precv.at[d - 1], send_sem=ps_sem.at[d - 1],
            recv_sem=pr_sem.at[d - 1], device_id={"curve": ci, "line": line_at(d)},
            device_id_type=MESH)
        copy.start()
        copies.append(copy)
    fetch_target.wait()
    ry = lax.broadcasted_iota(jnp.int32, (32, 512), 0)
    ly = lax.broadcasted_iota(jnp.int32, (32, 512), 1)
    spread = dot(tgt_ref[...], jnp.where((ly >> 4) == ry, 1.0, 0.0).astype(jnp.float32))
    rm = lax.broadcasted_iota(jnp.int32, (96, 512), 0)
    lm = lax.broadcasted_iota(jnp.int32, (96, 512), 1)
    spread = jnp.where((rm & 15) == (lm & 15), spread, 0.0)
    target = jnp.zeros((24, 128), jnp.float32)
    for yy in range(4):
        pick = jnp.logical_and((r24 >> 2) == (c96 >> 4), (r24 & 3) == yy)
        target = target + dot(jnp.where(pick, 1.0, 0.0).astype(jnp.float32),
                              spread[:, 128 * yy:128 * yy + 128])

    total = psend[...]
    for d in range(1, nl):
        copies[d - 1].wait_recv()
        total = total + precv[d - 1]

    misfit = 0.5 * (target - (2.0 / total_x) * total)
    wide = dot(gather, misfit, ((0,), (0,)))
    wide = wide * cos96 - swapped(wide) * sin96
    nudge = dot(wide, basis, ((1,), (1,)))

    for v in range(4):
        m = [g[v, pl.ds(8 * j, 8), :] for j in range(27)]
        powers = []
        for k in range(3):
            at = 8 * (4 * k + v)
            shifted = velocity[k][v] + nudge[at:at + 8, :]
            powers.append((None, shifted, shifted * shifted + 1.0 / 3.0))
        relaxed = []
        for a in range(3):
            along_a = m[0] if a == 0 else m[0] * powers[0][a]
            for b in range(3):
                along_b = along_a if b == 0 else along_a * powers[1][b]
                for c in range(3):
                    eq = along_b if c == 0 else along_b * powers[2][c]
                    j = 9 * a + 3 * b + c
                    relaxed.append(m[j] - rates[j] * (m[j] - eq))
        for stride in (1, 3, 9):
            relaxed = along(relaxed, stride, from_moments)
        for j in range(27):
            post[v, pl.ds(8 * j, 8), :] = relaxed[j]

    store = pltpu.make_async_copy(post, post_out, io_sem.at[2])
    store.start()

    def at(j, v):
        return post[v, pl.ds(8 * j, 8), :]

    halo = []
    for n, cy in enumerate((1, -1)):
        for cx in (-1, 0, 1):
            pack = solid
            for cz in range(3):
                for z in range(2):
                    c = 2 * cz + z
                    j = 9 * (cx + 1) + 3 * (cy + 1) + cz
                    if cy == 1:
                        moved = lroll(at(j, 2 * z + 1), 16 * c - 112)
                    else:
                        moved = lroll(at(j, 2 * z), 16 * c)
                    pack = jnp.where(chunk == c, moved, pack)
            ysend[n, cx + 1] = pack
        for e, cx in enumerate((1, -1)):
            halo.append(pltpu.make_async_remote_copy(
                src_ref=ysend.at[n, cx + 1], dst_ref=yside.at[n, e],
                send_sem=ds_sem.at[n, e], recv_sem=dr_sem.at[n, e],
                device_id={"curve": curve_at(cy), "line": line_at(cx)},
                device_id_type=MESH))
            halo[-1].start()
        halo.append(pltpu.make_async_remote_copy(
            src_ref=ysend.at[n], dst_ref=yrecv.at[n], send_sem=ys_sem.at[n],
            recv_sem=yr_sem.at[n], device_id={"curve": curve_at(cy), "line": li},
            device_id_type=MESH))
        halo[-1].start()
    for n, cx in enumerate((1, -1)):
        for v in range(4):
            pack = solid
            for k in range(9):
                moved = lroll(at(9 * (cx + 1) + k, v), k - 15 if cx == 1 else k)
                pack = jnp.where(q == k, moved, pack)
            xsend[n, v] = pack
        halo.append(pltpu.make_async_remote_copy(
            src_ref=xsend.at[n], dst_ref=xrecv.at[n], send_sem=xs_sem.at[n],
            recv_sem=xr_sem.at[n], device_id={"curve": ci, "line": line_at(cx)},
            device_id_type=MESH))
        halo[-1].start()
    for copy in halo:
        copy.wait_recv()

    def beside(own, other, cx):
        if cx == 1:
            return jnp.where(tx == 0, sroll(other, 5), sroll(own, 1))
        return jnp.where(tx == 3, sroll(other, 3), sroll(own, 7))

    def x_edge(cx):
        return q == (0 if cx == 1 else 15)

    for n, cy in enumerate((1, -1)):
        for cx in (-1, 0, 1):
            row = yrecv[n, cx + 1]
            if cx != 0:
                near = beside(row, yside[n, 0 if cx == 1 else 1], cx)
                row = jnp.where(x_edge(cx), lroll(near, -15 * cx), lroll(row, cx))
            rows_ref[n, cx + 1] = sroll(row, 4)
    for n, cx in enumerate((1, -1)):
        for v in range(4):
            cols_ref[n, v] = beside(xsend[n, v], xrecv[n, v], cx)
    for copy in copies + halo:
        copy.wait_send()
    store.wait()


def stream(keys, post, cols_ref, rows_ref, out, g, out_ref, sem):
    shape = (8, 128)
    lane = lax.broadcasted_iota(jnp.int32, shape, 1)
    sub = lax.broadcasted_iota(jnp.int32, shape, 0)
    q = lane & 15
    key = [keys[0, 0, s] for s in range(SLOTS)]

    present = sub == key[0]
    for s in range(1, SLOTS):
        present = jnp.logical_or(present, sub == key[s])
    solid = jnp.where(present, 0.0, 1.0).astype(jnp.float32)

    def at(j, v):
        return post[v, pl.ds(8 * j, 8), :]

    def x_edge(cx):
        return q == (0 if cx == 1 else 15)

    def step_x(own, cx, k, v):
        if cx == 0:
            return own
        near = lroll(cols_ref[0 if cx == 1 else 1, v], -k if cx == 1 else 15 - k)
        return jnp.where(x_edge(cx), near, lroll(own, cx))

    def step_y(a0, a1, cx, cy, c):
        if cy == 0:
            return a0, a1
        r0, r1 = lroll(a0, 16 * cy), lroll(a1, 16 * cy)
        if cy == 1:
            row = lroll(rows_ref[0 if cy == 1 else 1, cx + 1], -16 * c)
            row = jnp.where(sub < 4, row, sroll(r1, 4))
            return jnp.where(lane < 16, row, r0), jnp.where(lane < 16, r0, r1)
        row = lroll(rows_ref[0 if cy == 1 else 1, cx + 1], 112 - 16 * c)
        row = jnp.where(sub >= 4, row, sroll(r0, 4))
        return jnp.where(lane >= 112, r1, r0), jnp.where(lane >= 112, row, r1)

    for cx in (-1, 0, 1):
        for cy in (-1, 0, 1):
            base = 9 * (cx + 1) + 3 * (cy + 1)
            if cx == 0 and cy == 0:
                blocked = None
            else:
                wall = step_x(solid, cx, 9, 0)
                walls = step_y(wall, wall, cx, cy, 6)
                blocked = [w > 0.5 for w in walls]

            def moved(cz, z):
                j = base + cz
                k = 3 * (cy + 1) + cz
                a = [step_x(at(j, 2 * z + h), cx, k, 2 * z + h) for h in range(2)]
                return step_y(a[0], a[1], cx, cy, 2 * cz + z)

            def put(cz, z, source):
                j = base + cz
                for h in range(2):
                    value = at(26 - j, 2 * z + h)
                    if source is not None:
                        value = source[h] if blocked is None else jnp.where(blocked[h], value, source[h])
                    g[2 * z + h, pl.ds(8 * j, 8), :] = value

            put(1, 0, moved(1, 0))
            put(1, 1, moved(1, 1))
            put(2, 0, None)
            put(2, 1, moved(2, 0))
            put(0, 0, moved(0, 1))
            put(0, 1, moved(2, 1))

    writes = []
    for s in range(SLOTS):
        place = jnp.maximum(key[s], 0)
        keep = jnp.where(key[s] >= 0, 1.0, 0.0).astype(jnp.float32)
        for v in range(4):
            out_ref[pl.ds(108 * s + v, 27, stride=4), :] = g[v, pl.ds(place, 27, stride=8), :] * keep
        if s % 2 == 1:
            part = pl.ds(108 * (s - 1), 216)
            writes.append(pltpu.make_async_copy(out_ref.at[part], out.at[part], sem.at[s // 2]))
            writes[-1].start()
    for copy in writes:
        copy.wait()


def solution(mesh):
    nc, nl = mesh.shape["curve"], mesh.shape["line"]

    def on_device(scaled, places, waves, amplitudes, rates):
        x = scaled.reshape(SLOTS * 108, 128)
        target = amplitudes.transpose(0, 1, 3, 2).reshape(96, 32)
        vmem = pl.BlockSpec(memory_space=pltpu.VMEM)
        hbm = pl.BlockSpec(memory_space=pl.ANY)
        smem = pl.BlockSpec(memory_space=pltpu.SMEM)
        f32 = jnp.float32
        dma = pltpu.SemaphoreType.DMA
        post, cols, rows = pl.pallas_call(
            functools.partial(collide, nc, nl),
            out_shape=[
                jax.ShapeDtypeStruct((4, 216, 128), f32),
                jax.ShapeDtypeStruct((2, 4, 8, 128), f32),
                jax.ShapeDtypeStruct((2, 3, 8, 128), f32),
            ],
            in_specs=[smem, smem, smem, hbm, hbm],
            out_specs=[hbm, vmem, vmem],
            scratch_shapes=[
                pltpu.VMEM((SLOTS * 108, 128), f32),
                pltpu.VMEM((96, 32), f32),
                pltpu.VMEM((4, 216, 128), f32),
                pltpu.VMEM((4, 216, 128), f32),
                pltpu.VMEM((24, 128), f32),
                pltpu.VMEM((nl - 1, 24, 128), f32),
                pltpu.VMEM((2, 4, 8, 128), f32),
                pltpu.VMEM((2, 4, 8, 128), f32),
                pltpu.VMEM((2, 3, 8, 128), f32),
                pltpu.VMEM((2, 3, 8, 128), f32),
                pltpu.VMEM((2, 2, 8, 128), f32),
                dma((nl - 1,)), dma((nl - 1,)),
                dma((2,)), dma((2,)), dma((2,)), dma((2,)),
                dma((2, 2)), dma((2, 2)), dma((3,)),
            ],
            compiler_params=pltpu.CompilerParams(collective_id=0, has_side_effects=True),
        )(places, waves, rates, x, target)
        out = pl.pallas_call(
            stream,
            out_shape=jax.ShapeDtypeStruct((SLOTS * 108, 128), f32),
            in_specs=[smem, vmem, vmem, vmem],
            out_specs=hbm,
            scratch_shapes=[
                pltpu.VMEM((4, 216, 128), f32),
                pltpu.VMEM((SLOTS * 108, 128), f32),
                dma((SLOTS // 2,)),
            ],
        )(places, post, cols, rows)
        return out.reshape(1, 1, SLOTS, 27, 512)

    return jax.shard_map(
        on_device,
        mesh=mesh,
        in_specs=(
            P("curve", "line", None, None, None),
            P("curve", "line", None),
            P(),
            P(None, None, "curve", None),
            P(),
        ),
        out_specs=P("curve", "line", None, None, None),
        check_vma=False,
    )
```

```python
import functools

import jax
import jax.numpy as jnp
import numpy as np
from jax import lax
from jax.experimental import pallas as pl
from jax.experimental.pallas import tpu as pltpu
from jax.sharding import PartitionSpec as P

SLOTS = 6
MESH = pl.DeviceIdType.MESH
TWO_PI = 6.283185307179586
HIGHEST = lax.Precision.HIGHEST


def along(items, stride, fn):
    done = list(items)
    for base in range(27):
        if (base // stride) % 3 == 0:
            at = (base, base + stride, base + 2 * stride)
            got = fn(*(items[n] for n in at))
            for n, value in zip(at, got):
                done[n] = value
    return done


def to_moments(low, mid, high):
    both = (low + high) * (1.0 / 6.0)
    return both + mid * (2.0 / 3.0), (high - low) * (1.0 / 6.0), both


def from_moments(m0, m1, m2):
    return (m2 - m1) * 3.0, (m0 - m2) * 1.5, (m1 + m2) * 3.0


def dot(a, b, dims=((1,), (0,))):
    return lax.dot_general(a, b, (dims, ((), ())), precision=HIGHEST,
                           preferred_element_type=jnp.float32)


def lroll(x, shift):
    shift = shift % 128
    return x if shift == 0 else pltpu.roll(x, shift, 1)


def sroll(x, shift):
    return pltpu.roll(x, shift % 8, 0)


def collide(nc, nl, keys, waves, rates, x_in, tgt_in, post, cols_ref, rows_ref,
            x_ref, tgt_ref, g, psend, precv, xsend, xrecv, ysend, yrecv, yside,
           ps_sem, pr_sem, xs_sem, xr_sem, ys_sem, yr_sem, ds_sem, dr_sem, io_sem):
    ci = lax.axis_index("curve")
    li = lax.axis_index("line")

    fetch = pltpu.make_async_copy(x_in, x_ref, io_sem.at[0])
    fetch.start()
    fetch_target = pltpu.make_async_copy(tgt_in, tgt_ref, io_sem.at[1])
    fetch_target.start()

    def line_at(d):
        return lax.rem(li + (d + nl), nl)

    def curve_at(d):
        return lax.rem(ci + (d + nc), nc)

    barrier = pltpu.get_barrier_semaphore()
    friends = [{"curve": ci, "line": line_at(d)} for d in range(1, nl)]
    friends += [{"curve": curve_at(dy), "line": line_at(dx)} for dy in (-1, 1) for dx in (-1, 0, 1)]
    for friend in friends:
        pl.semaphore_signal(barrier, inc=1, device_id=friend, device_id_type=MESH)

    shape = (8, 128)
    lane = lax.broadcasted_iota(jnp.int32, shape, 1)
    sub = lax.broadcasted_iota(jnp.int32, shape, 0)
    q = lane & 15
    chunk = lane >> 4
    tx = sub & 3
    key = [keys[0, 0, s] for s in range(SLOTS)]

    present = sub == key[0]
    for s in range(1, SLOTS):
        present = jnp.logical_or(present, sub == key[s])
    fluid = jnp.where(present, 1.0, 0.0).astype(jnp.float32)
    solid = 1.0 - fluid

    def wave_lanes(ids):
        m = ids & 7
        out = jnp.full(ids.shape, waves[0], jnp.int32)
        for n in range(1, 8):
            out = jnp.where(m == n, waves[n], out)
        return out

    total_x = nl * 64
    unit = TWO_PI / total_x
    lane16 = lax.broadcasted_iota(jnp.int32, (16, 128), 1)
    row16 = lax.broadcasted_iota(jnp.int32, (16, 128), 0)
    turn = lax.rem(wave_lanes(lane16) * row16, total_x)
    turn = jnp.where((lane16 & 15) >= 8, turn - total_x // 4, turn)
    small = jnp.cos(turn.astype(jnp.float32) * unit)
    rowb = lax.broadcasted_iota(jnp.int32, (128, 128), 0)
    laneb = lax.broadcasted_iota(jnp.int32, (128, 128), 1)
    basis = jnp.where((rowb >> 4) == (laneb >> 4), jnp.concatenate([small] * 8, axis=0), 0.0)

    start = lax.rem(wave_lanes(lane) * ((li * 4 + tx) * 16), total_x)
    angle = start.astype(jnp.float32) * unit
    cos0 = jnp.cos(angle)
    sin0 = jnp.cos((start - total_x // 4).astype(jnp.float32) * unit)
    is_sin = q >= 8
    sin_signed = jnp.where(is_sin, sin0, -sin0)
    cos96 = jnp.concatenate([cos0] * 12, axis=0)
    sin96 = jnp.concatenate([sin_signed] * 12, axis=0)
    is_sin96 = (lax.broadcasted_iota(jnp.int32, (96, 128), 1) & 15) >= 8

    def swapped(t):
        return jnp.where(is_sin96, pltpu.roll(t, 8, 1), pltpu.roll(t, 120, 1))

    r24 = lax.broadcasted_iota(jnp.int32, (24, 96), 0)
    c96 = lax.broadcasted_iota(jnp.int32, (24, 96), 1)
    same = (r24 >> 2) == (c96 >> 4)
    same = jnp.logical_and(same, ((r24 >> 1) & 1) == ((c96 >> 2) & 1))
    same = jnp.logical_and(same, (r24 & 1) == ((c96 >> 3) & 1))
    gather = jnp.where(same, 1.0, 0.0).astype(jnp.float32)

    fetch.wait()
    for p in range(8):
        slot = jnp.int32(0)
        for s in range(SLOTS):
            slot = jnp.where(key[s] == p, s, slot)
        for v in range(4):
            g[v, pl.ds(p, 27, stride=8), :] = x_ref[pl.ds(slot * 108 + v, 27, stride=4), :]

    velocity = [[None] * 4 for _ in range(3)]
    for v in range(4):
        f = [g[v, pl.ds(8 * j, 8), :] for j in range(27)]
        for stride in (1, 3, 9):
            f = along(f, stride, to_moments)
        for j in range(27):
            g[v, pl.ds(8 * j, 8), :] = f[j]
        scale = fluid / f[0]
        for k, j in enumerate((9, 3, 1)):
            velocity[k][v] = f[j] * scale

    stack = jnp.concatenate([velocity[k][v] for k in range(3) for v in range(4)], axis=0)
    local = dot(stack, basis)
    local = local * cos96 + swapped(local) * sin96
    psend[...] = dot(gather, local)

    pl.semaphore_wait(barrier, len(friends))

    copies = []
    for d in range(1, nl):
        copy = pltpu.make_async_remote_copy(
            src_ref=psend, dst_ref=precv.at[d - 1], send_sem=ps_sem.at[d - 1],
            recv_sem=pr_sem.at[d - 1], device_id={"curve": ci, "line": line_at(d)},
            device_id_type=MESH)
        copy.start()
        copies.append(copy)
    fetch_target.wait()
    ry = lax.broadcasted_iota(jnp.int32, (32, 512), 0)
    ly = lax.broadcasted_iota(jnp.int32, (32, 512), 1)
    spread = dot(tgt_ref[...], jnp.where((ly >> 4) == ry, 1.0, 0.0).astype(jnp.float32))
    rm = lax.broadcasted_iota(jnp.int32, (96, 512), 0)
    lm = lax.broadcasted_iota(jnp.int32, (96, 512), 1)
    spread = jnp.where((rm & 15) == (lm & 15), spread, 0.0)
    target = jnp.zeros((24, 128), jnp.float32)
    for yy in range(4):
        pick = jnp.logical_and((r24 >> 2) == (c96 >> 4), (r24 & 3) == yy)
        target = target + dot(jnp.where(pick, 1.0, 0.0).astype(jnp.float32),
                              spread[:, 128 * yy:128 * yy + 128])

    total = psend[...]
    for d in range(1, nl):
        copies[d - 1].wait_recv()
        total = total + precv[d - 1]

    misfit = 0.5 * (target - (2.0 / total_x) * total)
    wide = dot(gather, misfit, ((0,), (0,)))
    wide = wide * cos96 - swapped(wide) * sin96
    nudge = dot(wide, basis, ((1,), (1,)))

    for v in range(4):
        m = [g[v, pl.ds(8 * j, 8), :] for j in range(27)]
        powers = []
        for k in range(3):
            at = 8 * (4 * k + v)
            shifted = velocity[k][v] + nudge[at:at + 8, :]
            powers.append((None, shifted, shifted * shifted + 1.0 / 3.0))
        relaxed = []
        for a in range(3):
            along_a = m[0] if a == 0 else m[0] * powers[0][a]
            for b in range(3):
                along_b = along_a if b == 0 else along_a * powers[1][b]
                for c in range(3):
                    eq = along_b if c == 0 else along_b * powers[2][c]
                    j = 9 * a + 3 * b + c
                    relaxed.append(m[j] - rates[j] * (m[j] - eq))
        for stride in (1, 3, 9):
            relaxed = along(relaxed, stride, from_moments)
        for j in range(27):
            post[v, pl.ds(8 * j, 8), :] = relaxed[j]

    def at(j, v):
        return post[v, pl.ds(8 * j, 8), :]

    halo = []
    for n, cy in enumerate((1, -1)):
        for cx in (-1, 0, 1):
            pack = solid
            for cz in range(3):
                for z in range(2):
                    c = 2 * cz + z
                    j = 9 * (cx + 1) + 3 * (cy + 1) + cz
                    if cy == 1:
                        moved = lroll(at(j, 2 * z + 1), 16 * c - 112)
                    else:
                        moved = lroll(at(j, 2 * z), 16 * c)
                    pack = jnp.where(chunk == c, moved, pack)
            ysend[n, cx + 1] = pack
        for e, cx in enumerate((1, -1)):
            halo.append(pltpu.make_async_remote_copy(
                src_ref=ysend.at[n, cx + 1], dst_ref=yside.at[n, e],
                send_sem=ds_sem.at[n, e], recv_sem=dr_sem.at[n, e],
                device_id={"curve": curve_at(cy), "line": line_at(cx)},
                device_id_type=MESH))
            halo[-1].start()
        halo.append(pltpu.make_async_remote_copy(
            src_ref=ysend.at[n], dst_ref=yrecv.at[n], send_sem=ys_sem.at[n],
            recv_sem=yr_sem.at[n], device_id={"curve": curve_at(cy), "line": li},
            device_id_type=MESH))
        halo[-1].start()
    for n, cx in enumerate((1, -1)):
        for v in range(4):
            pack = solid
            for k in range(9):
                moved = lroll(at(9 * (cx + 1) + k, v), k - 15 if cx == 1 else k)
                pack = jnp.where(q == k, moved, pack)
            xsend[n, v] = pack
        halo.append(pltpu.make_async_remote_copy(
            src_ref=xsend.at[n], dst_ref=xrecv.at[n], send_sem=xs_sem.at[n],
            recv_sem=xr_sem.at[n], device_id={"curve": ci, "line": line_at(cx)},
            device_id_type=MESH))
        halo[-1].start()
    for copy in halo:
        copy.wait_recv()

    def beside(own, other, cx):
        if cx == 1:
            return jnp.where(tx == 0, sroll(other, 5), sroll(own, 1))
        return jnp.where(tx == 3, sroll(other, 3), sroll(own, 7))

    def x_edge(cx):
        return q == (0 if cx == 1 else 15)

    for n, cy in enumerate((1, -1)):
        for cx in (-1, 0, 1):
            row = yrecv[n, cx + 1]
            if cx != 0:
                near = beside(row, yside[n, 0 if cx == 1 else 1], cx)
                row = jnp.where(x_edge(cx), lroll(near, -15 * cx), lroll(row, cx))
            rows_ref[n, cx + 1] = sroll(row, 4)
    for n, cx in enumerate((1, -1)):
        for v in range(4):
            cols_ref[n, v] = beside(xsend[n, v], xrecv[n, v], cx)
    for copy in copies + halo:
        copy.wait_send()


def stream(keys, post, cols_ref, rows_ref, out, g, out_ref, sem):
    shape = (8, 128)
    lane = lax.broadcasted_iota(jnp.int32, shape, 1)
    sub = lax.broadcasted_iota(jnp.int32, shape, 0)
    q = lane & 15
    key = [keys[0, 0, s] for s in range(SLOTS)]

    present = sub == key[0]
    for s in range(1, SLOTS):
        present = jnp.logical_or(present, sub == key[s])
    solid = jnp.where(present, 0.0, 1.0).astype(jnp.float32)

    def at(j, v):
        return post[v, pl.ds(8 * j, 8), :]

    def x_edge(cx):
        return q == (0 if cx == 1 else 15)

    def step_x(own, cx, k, v):
        if cx == 0:
            return own
        near = lroll(cols_ref[0 if cx == 1 else 1, v], -k if cx == 1 else 15 - k)
        return jnp.where(x_edge(cx), near, lroll(own, cx))

    def step_y(a0, a1, cx, cy, c):
        if cy == 0:
            return a0, a1
        r0, r1 = lroll(a0, 16 * cy), lroll(a1, 16 * cy)
        if cy == 1:
            row = lroll(rows_ref[0 if cy == 1 else 1, cx + 1], -16 * c)
            row = jnp.where(sub < 4, row, sroll(r1, 4))
            return jnp.where(lane < 16, row, r0), jnp.where(lane < 16, r0, r1)
        row = lroll(rows_ref[0 if cy == 1 else 1, cx + 1], 112 - 16 * c)
        row = jnp.where(sub >= 4, row, sroll(r0, 4))
        return jnp.where(lane >= 112, r1, r0), jnp.where(lane >= 112, row, r1)

    for cx in (-1, 0, 1):
        for cy in (-1, 0, 1):
            base = 9 * (cx + 1) + 3 * (cy + 1)
            if cx == 0 and cy == 0:
                blocked = None
            else:
                wall = step_x(solid, cx, 9, 0)
                walls = step_y(wall, wall, cx, cy, 6)
                blocked = [w > 0.5 for w in walls]

            def moved(cz, z):
                j = base + cz
                k = 3 * (cy + 1) + cz
                a = [step_x(at(j, 2 * z + h), cx, k, 2 * z + h) for h in range(2)]
                return step_y(a[0], a[1], cx, cy, 2 * cz + z)

            def put(cz, z, source):
                j = base + cz
                for h in range(2):
                    value = at(26 - j, 2 * z + h)
                    if source is not None:
                        value = source[h] if blocked is None else jnp.where(blocked[h], value, source[h])
                    g[2 * z + h, pl.ds(8 * j, 8), :] = value

            put(1, 0, moved(1, 0))
            put(1, 1, moved(1, 1))
            put(2, 0, None)
            put(2, 1, moved(2, 0))
            put(0, 0, moved(0, 1))
            put(0, 1, moved(2, 1))

    writes = []
    for s in range(SLOTS):
        place = jnp.maximum(key[s], 0)
        keep = jnp.where(key[s] >= 0, 1.0, 0.0).astype(jnp.float32)
        for v in range(4):
            out_ref[pl.ds(108 * s + v, 27, stride=4), :] = g[v, pl.ds(place, 27, stride=8), :] * keep
        if s % 2 == 1:
            part = pl.ds(108 * (s - 1), 216)
            writes.append(pltpu.make_async_copy(out_ref.at[part], out.at[part], sem.at[s // 2]))
            writes[-1].start()
    for copy in writes:
        copy.wait()


def solution(mesh):
    nc, nl = mesh.shape["curve"], mesh.shape["line"]

    def on_device(scaled, places, waves, amplitudes, rates):
        x = scaled.reshape(SLOTS * 108, 128)
        target = amplitudes.transpose(0, 1, 3, 2).reshape(96, 32)
        vmem = pl.BlockSpec(memory_space=pltpu.VMEM)
        hbm = pl.BlockSpec(memory_space=pl.ANY)
        smem = pl.BlockSpec(memory_space=pltpu.SMEM)
        f32 = jnp.float32
        dma = pltpu.SemaphoreType.DMA
        post, cols, rows = pl.pallas_call(
            functools.partial(collide, nc, nl),
            out_shape=[
                pltpu.VMEM((4, 216, 128), f32),
                pltpu.VMEM((2, 4, 8, 128), f32),
                pltpu.VMEM((2, 3, 8, 128), f32),
            ],
            in_specs=[smem, smem, smem, hbm, hbm],
            out_specs=[vmem] * 3,
            scratch_shapes=[
                pltpu.VMEM((SLOTS * 108, 128), f32),
                pltpu.VMEM((96, 32), f32),
                pltpu.VMEM((4, 216, 128), f32),
                pltpu.VMEM((24, 128), f32),
                pltpu.VMEM((nl - 1, 24, 128), f32),
                pltpu.VMEM((2, 4, 8, 128), f32),
                pltpu.VMEM((2, 4, 8, 128), f32),
                pltpu.VMEM((2, 3, 8, 128), f32),
                pltpu.VMEM((2, 3, 8, 128), f32),
                pltpu.VMEM((2, 2, 8, 128), f32),
                dma((nl - 1,)), dma((nl - 1,)),
                dma((2,)), dma((2,)), dma((2,)), dma((2,)),
                dma((2, 2)), dma((2, 2)), dma((2,)),
            ],
            compiler_params=pltpu.CompilerParams(collective_id=0, has_side_effects=True),
        )(places, waves, rates, x, target)
        post, cols, rows = (
            pltpu.with_memory_space_constraint(a, pltpu.VMEM) for a in (post, cols, rows))
        out = pl.pallas_call(
            stream,
            out_shape=jax.ShapeDtypeStruct((SLOTS * 108, 128), f32),
            in_specs=[smem, vmem, vmem, vmem],
            out_specs=hbm,
            scratch_shapes=[
                pltpu.VMEM((4, 216, 128), f32),
                pltpu.VMEM((SLOTS * 108, 128), f32),
                dma((SLOTS // 2,)),
            ],
        )(places, post, cols, rows)
        return out.reshape(1, 1, SLOTS, 27, 512)

    return jax.shard_map(
        on_device,
        mesh=mesh,
        in_specs=(
            P("curve", "line", None, None, None),
            P("curve", "line", None),
            P(),
            P(None, None, "curve", None),
            P(),
        ),
        out_specs=P("curve", "line", None, None, None),
        check_vma=False,
    )
```

```python
import functools

import jax
import jax.numpy as jnp
import numpy as np
from jax import lax
from jax.experimental import pallas as pl
from jax.experimental.pallas import tpu as pltpu
from jax.sharding import PartitionSpec as P

SLOTS = 6
MESH = pl.DeviceIdType.MESH
TWO_PI = 6.283185307179586
HIGHEST = lax.Precision.HIGHEST


def along(items, stride, fn):
    done = list(items)
    for base in range(27):
        if (base // stride) % 3 == 0:
            at = (base, base + stride, base + 2 * stride)
            got = fn(*(items[n] for n in at))
            for n, value in zip(at, got):
                done[n] = value
    return done


def to_moments(low, mid, high):
    both = (low + high) * (1.0 / 6.0)
    return both + mid * (2.0 / 3.0), (high - low) * (1.0 / 6.0), both


def from_moments(m0, m1, m2):
    return (m2 - m1) * 3.0, (m0 - m2) * 1.5, (m1 + m2) * 3.0


def dot(a, b, dims=((1,), (0,))):
    return lax.dot_general(a, b, (dims, ((), ())), precision=HIGHEST,
                           preferred_element_type=jnp.float32)


def lroll(x, shift):
    shift = shift % 128
    return x if shift == 0 else pltpu.roll(x, shift, 1)


def sroll(x, shift):
    return pltpu.roll(x, shift % 8, 0)


def collide(nc, nl, keys, waves, rates, x_in, tgt_in, post, cols_ref, rows_ref,
            x_ref, tgt_ref, g, psend, precv, xsend, xmsg, xrecv, ysend, yrecv, yside,
           ps_sem, pr_sem, xs_sem, xr_sem, ys_sem, yr_sem, ds_sem, dr_sem, io_sem):
    ci = lax.axis_index("curve")
    li = lax.axis_index("line")

    fetch = pltpu.make_async_copy(x_in, x_ref, io_sem.at[0])
    fetch.start()
    fetch_target = pltpu.make_async_copy(tgt_in, tgt_ref, io_sem.at[1])
    fetch_target.start()

    def line_at(d):
        return lax.rem(li + (d + nl), nl)

    def curve_at(d):
        return lax.rem(ci + (d + nc), nc)

    barrier = pltpu.get_barrier_semaphore()
    friends = [{"curve": ci, "line": line_at(d)} for d in range(1, nl)]
    friends += [{"curve": curve_at(dy), "line": line_at(dx)} for dy in (-1, 1) for dx in (-1, 0, 1)]
    for friend in friends:
        pl.semaphore_signal(barrier, inc=1, device_id=friend, device_id_type=MESH)

    shape = (8, 128)
    lane = lax.broadcasted_iota(jnp.int32, shape, 1)
    sub = lax.broadcasted_iota(jnp.int32, shape, 0)
    q = lane & 15
    chunk = lane >> 4
    tx = sub & 3
    key = [keys[0, 0, s] for s in range(SLOTS)]

    present = sub == key[0]
    for s in range(1, SLOTS):
        present = jnp.logical_or(present, sub == key[s])
    fluid = jnp.where(present, 1.0, 0.0).astype(jnp.float32)
    solid = 1.0 - fluid

    def wave_lanes(ids):
        m = ids & 7
        out = jnp.full(ids.shape, waves[0], jnp.int32)
        for n in range(1, 8):
            out = jnp.where(m == n, waves[n], out)
        return out

    total_x = nl * 64
    unit = TWO_PI / total_x
    lane16 = lax.broadcasted_iota(jnp.int32, (16, 128), 1)
    row16 = lax.broadcasted_iota(jnp.int32, (16, 128), 0)
    turn = lax.rem(wave_lanes(lane16) * row16, total_x)
    turn = jnp.where((lane16 & 15) >= 8, turn - total_x // 4, turn)
    small = jnp.cos(turn.astype(jnp.float32) * unit)
    rowb = lax.broadcasted_iota(jnp.int32, (128, 128), 0)
    laneb = lax.broadcasted_iota(jnp.int32, (128, 128), 1)
    basis = jnp.where((rowb >> 4) == (laneb >> 4), jnp.concatenate([small] * 8, axis=0), 0.0)

    start = lax.rem(wave_lanes(lane) * ((li * 4 + tx) * 16), total_x)
    angle = start.astype(jnp.float32) * unit
    cos0 = jnp.cos(angle)
    sin0 = jnp.cos((start - total_x // 4).astype(jnp.float32) * unit)
    is_sin = q >= 8
    sin_signed = jnp.where(is_sin, sin0, -sin0)
    cos96 = jnp.concatenate([cos0] * 12, axis=0)
    sin96 = jnp.concatenate([sin_signed] * 12, axis=0)
    is_sin96 = (lax.broadcasted_iota(jnp.int32, (96, 128), 1) & 15) >= 8

    def swapped(t):
        return jnp.where(is_sin96, pltpu.roll(t, 8, 1), pltpu.roll(t, 120, 1))

    r24 = lax.broadcasted_iota(jnp.int32, (24, 96), 0)
    c96 = lax.broadcasted_iota(jnp.int32, (24, 96), 1)
    same = (r24 >> 2) == (c96 >> 4)
    same = jnp.logical_and(same, ((r24 >> 1) & 1) == ((c96 >> 2) & 1))
    same = jnp.logical_and(same, (r24 & 1) == ((c96 >> 3) & 1))
    gather = jnp.where(same, 1.0, 0.0).astype(jnp.float32)

    fetch.wait()
    for p in range(8):
        slot = jnp.int32(0)
        for s in range(SLOTS):
            slot = jnp.where(key[s] == p, s, slot)
        for v in range(4):
            g[v, pl.ds(p, 27, stride=8), :] = x_ref[pl.ds(slot * 108 + v, 27, stride=4), :]

    velocity = [[None] * 4 for _ in range(3)]
    for v in range(4):
        f = [g[v, pl.ds(8 * j, 8), :] for j in range(27)]
        for stride in (1, 3, 9):
            f = along(f, stride, to_moments)
        for j in range(27):
            g[v, pl.ds(8 * j, 8), :] = f[j]
        scale = fluid / f[0]
        for k, j in enumerate((9, 3, 1)):
            velocity[k][v] = f[j] * scale

    stack = jnp.concatenate([velocity[k][v] for k in range(3) for v in range(4)], axis=0)
    local = dot(stack, basis)
    local = local * cos96 + swapped(local) * sin96
    psend[...] = dot(gather, local)

    pl.semaphore_wait(barrier, len(friends))

    copies = []
    for d in range(1, nl):
        copy = pltpu.make_async_remote_copy(
            src_ref=psend, dst_ref=precv.at[d - 1], send_sem=ps_sem.at[d - 1],
            recv_sem=pr_sem.at[d - 1], device_id={"curve": ci, "line": line_at(d)},
            device_id_type=MESH)
        copy.start()
        copies.append(copy)
    fetch_target.wait()
    ry = lax.broadcasted_iota(jnp.int32, (32, 512), 0)
    ly = lax.broadcasted_iota(jnp.int32, (32, 512), 1)
    spread = dot(tgt_ref[...], jnp.where((ly >> 4) == ry, 1.0, 0.0).astype(jnp.float32))
    rm = lax.broadcasted_iota(jnp.int32, (96, 512), 0)
    lm = lax.broadcasted_iota(jnp.int32, (96, 512), 1)
    spread = jnp.where((rm & 15) == (lm & 15), spread, 0.0)
    target = jnp.zeros((24, 128), jnp.float32)
    for yy in range(4):
        pick = jnp.logical_and((r24 >> 2) == (c96 >> 4), (r24 & 3) == yy)
        target = target + dot(jnp.where(pick, 1.0, 0.0).astype(jnp.float32),
                              spread[:, 128 * yy:128 * yy + 128])

    total = psend[...]
    for d in range(1, nl):
        copies[d - 1].wait_recv()
        total = total + precv[d - 1]

    misfit = 0.5 * (target - (2.0 / total_x) * total)
    wide = dot(gather, misfit, ((0,), (0,)))
    wide = wide * cos96 - swapped(wide) * sin96
    nudge = dot(wide, basis, ((1,), (1,)))

    for v in range(4):
        m = [g[v, pl.ds(8 * j, 8), :] for j in range(27)]
        powers = []
        for k in range(3):
            at = 8 * (4 * k + v)
            shifted = velocity[k][v] + nudge[at:at + 8, :]
            powers.append((None, shifted, shifted * shifted + 1.0 / 3.0))
        relaxed = []
        for a in range(3):
            along_a = m[0] if a == 0 else m[0] * powers[0][a]
            for b in range(3):
                along_b = along_a if b == 0 else along_a * powers[1][b]
                for c in range(3):
                    eq = along_b if c == 0 else along_b * powers[2][c]
                    j = 9 * a + 3 * b + c
                    relaxed.append(m[j] - rates[j] * (m[j] - eq))
        for stride in (1, 3, 9):
            relaxed = along(relaxed, stride, from_moments)
        for j in range(27):
            post[v, pl.ds(8 * j, 8), :] = relaxed[j]

    def at(j, v):
        return post[v, pl.ds(8 * j, 8), :]

    halo = []
    for n, cy in enumerate((1, -1)):
        for cx in (-1, 0, 1):
            pack = solid
            for cz in range(3):
                for z in range(2):
                    c = 2 * cz + z
                    j = 9 * (cx + 1) + 3 * (cy + 1) + cz
                    if cy == 1:
                        moved = lroll(at(j, 2 * z + 1), 16 * c - 112)
                    else:
                        moved = lroll(at(j, 2 * z), 16 * c)
                    pack = jnp.where(chunk == c, moved, pack)
            ysend[n, cx + 1] = pack
        for e, cx in enumerate((1, -1)):
            halo.append(pltpu.make_async_remote_copy(
                src_ref=ysend.at[n, cx + 1], dst_ref=yside.at[n, e],
                send_sem=ds_sem.at[n, e], recv_sem=dr_sem.at[n, e],
                device_id={"curve": curve_at(cy), "line": line_at(cx)},
                device_id_type=MESH))
            halo[-1].start()
        halo.append(pltpu.make_async_remote_copy(
            src_ref=ysend.at[n], dst_ref=yrecv.at[n], send_sem=ys_sem.at[n],
            recv_sem=yr_sem.at[n], device_id={"curve": curve_at(cy), "line": li},
            device_id_type=MESH))
        halo[-1].start()
    for n, cx in enumerate((1, -1)):
        merged = jnp.zeros(shape, jnp.float32)
        for v in range(4):
            pack = solid
            for k in range(9):
                moved = lroll(at(9 * (cx + 1) + k, v), k - 15 if cx == 1 else k)
                pack = jnp.where(q == k, moved, pack)
            xsend[n, v] = pack
            merged = jnp.where(tx == v, sroll(pack, v - 3 if cx == 1 else v), merged)
        xmsg[n] = merged
        halo.append(pltpu.make_async_remote_copy(
            src_ref=xmsg.at[n], dst_ref=xrecv.at[n], send_sem=xs_sem.at[n],
            recv_sem=xr_sem.at[n], device_id={"curve": ci, "line": line_at(cx)},
            device_id_type=MESH))
        halo[-1].start()
    for copy in halo:
        copy.wait_recv()

    def beside(own, other, cx):
        if cx == 1:
            return jnp.where(tx == 0, sroll(other, 5), sroll(own, 1))
        return jnp.where(tx == 3, sroll(other, 3), sroll(own, 7))

    def x_edge(cx):
        return q == (0 if cx == 1 else 15)

    for n, cy in enumerate((1, -1)):
        for cx in (-1, 0, 1):
            row = yrecv[n, cx + 1]
            if cx != 0:
                near = beside(row, yside[n, 0 if cx == 1 else 1], cx)
                row = jnp.where(x_edge(cx), lroll(near, -15 * cx), lroll(row, cx))
            rows_ref[n, cx + 1] = sroll(row, 4)
    for n, cx in enumerate((1, -1)):
        for v in range(4):
            own, other = xsend[n, v], xrecv[n]
            if cx == 1:
                cols_ref[n, v] = jnp.where(tx == 0, sroll(other, -v), sroll(own, 1))
            else:
                cols_ref[n, v] = jnp.where(tx == 3, sroll(other, 3 - v), sroll(own, 7))
    for copy in copies + halo:
        copy.wait_send()


def stream(keys, post, cols_ref, rows_ref, out, g, out_ref, sem):
    shape = (8, 128)
    lane = lax.broadcasted_iota(jnp.int32, shape, 1)
    sub = lax.broadcasted_iota(jnp.int32, shape, 0)
    q = lane & 15
    key = [keys[0, 0, s] for s in range(SLOTS)]

    present = sub == key[0]
    for s in range(1, SLOTS):
        present = jnp.logical_or(present, sub == key[s])
    solid = jnp.where(present, 0.0, 1.0).astype(jnp.float32)

    def at(j, v):
        return post[v, pl.ds(8 * j, 8), :]

    def x_edge(cx):
        return q == (0 if cx == 1 else 15)

    def step_x(own, cx, k, v):
        if cx == 0:
            return own
        near = lroll(cols_ref[0 if cx == 1 else 1, v], -k if cx == 1 else 15 - k)
        return jnp.where(x_edge(cx), near, lroll(own, cx))

    def step_y(a0, a1, cx, cy, c):
        if cy == 0:
            return a0, a1
        r0, r1 = lroll(a0, 16 * cy), lroll(a1, 16 * cy)
        if cy == 1:
            row = lroll(rows_ref[0 if cy == 1 else 1, cx + 1], -16 * c)
            row = jnp.where(sub < 4, row, sroll(r1, 4))
            return jnp.where(lane < 16, row, r0), jnp.where(lane < 16, r0, r1)
        row = lroll(rows_ref[0 if cy == 1 else 1, cx + 1], 112 - 16 * c)
        row = jnp.where(sub >= 4, row, sroll(r0, 4))
        return jnp.where(lane >= 112, r1, r0), jnp.where(lane >= 112, row, r1)

    for cx in (-1, 0, 1):
        for cy in (-1, 0, 1):
            base = 9 * (cx + 1) + 3 * (cy + 1)
            if cx == 0 and cy == 0:
                blocked = None
            else:
                wall = step_x(solid, cx, 9, 0)
                walls = step_y(wall, wall, cx, cy, 6)
                blocked = [w > 0.5 for w in walls]

            def moved(cz, z):
                j = base + cz
                k = 3 * (cy + 1) + cz
                a = [step_x(at(j, 2 * z + h), cx, k, 2 * z + h) for h in range(2)]
                return step_y(a[0], a[1], cx, cy, 2 * cz + z)

            def put(cz, z, source):
                j = base + cz
                for h in range(2):
                    value = at(26 - j, 2 * z + h)
                    if source is not None:
                        value = source[h] if blocked is None else jnp.where(blocked[h], value, source[h])
                    g[2 * z + h, pl.ds(8 * j, 8), :] = value

            put(1, 0, moved(1, 0))
            put(1, 1, moved(1, 1))
            put(2, 0, None)
            put(2, 1, moved(2, 0))
            put(0, 0, moved(0, 1))
            put(0, 1, moved(2, 1))

    writes = []
    for s in range(SLOTS):
        place = jnp.maximum(key[s], 0)
        keep = jnp.where(key[s] >= 0, 1.0, 0.0).astype(jnp.float32)
        for v in range(4):
            out_ref[pl.ds(108 * s + v, 27, stride=4), :] = g[v, pl.ds(place, 27, stride=8), :] * keep
        if s % 2 == 1:
            part = pl.ds(108 * (s - 1), 216)
            writes.append(pltpu.make_async_copy(out_ref.at[part], out.at[part], sem.at[s // 2]))
            writes[-1].start()
    for copy in writes:
        copy.wait()


def solution(mesh):
    nc, nl = mesh.shape["curve"], mesh.shape["line"]

    def on_device(scaled, places, waves, amplitudes, rates):
        x = scaled.reshape(SLOTS * 108, 128)
        target = amplitudes.transpose(0, 1, 3, 2).reshape(96, 32)
        vmem = pl.BlockSpec(memory_space=pltpu.VMEM)
        hbm = pl.BlockSpec(memory_space=pl.ANY)
        smem = pl.BlockSpec(memory_space=pltpu.SMEM)
        f32 = jnp.float32
        dma = pltpu.SemaphoreType.DMA
        post, cols, rows = pl.pallas_call(
            functools.partial(collide, nc, nl),
            out_shape=[
                pltpu.VMEM((4, 216, 128), f32),
                pltpu.VMEM((2, 4, 8, 128), f32),
                pltpu.VMEM((2, 3, 8, 128), f32),
            ],
            in_specs=[smem, smem, smem, hbm, hbm],
            out_specs=[vmem] * 3,
            scratch_shapes=[
                pltpu.VMEM((SLOTS * 108, 128), f32),
                pltpu.VMEM((96, 32), f32),
                pltpu.VMEM((4, 216, 128), f32),
                pltpu.VMEM((24, 128), f32),
                pltpu.VMEM((nl - 1, 24, 128), f32),
                pltpu.VMEM((2, 4, 8, 128), f32),
                pltpu.VMEM((2, 8, 128), f32),
                pltpu.VMEM((2, 8, 128), f32),
                pltpu.VMEM((2, 3, 8, 128), f32),
                pltpu.VMEM((2, 3, 8, 128), f32),
                pltpu.VMEM((2, 2, 8, 128), f32),
                dma((nl - 1,)), dma((nl - 1,)),
                dma((2,)), dma((2,)), dma((2,)), dma((2,)),
                dma((2, 2)), dma((2, 2)), dma((2,)),
            ],
            compiler_params=pltpu.CompilerParams(collective_id=0, has_side_effects=True),
        )(places, waves, rates, x, target)
        post, cols, rows = (
            pltpu.with_memory_space_constraint(a, pltpu.VMEM) for a in (post, cols, rows))
        out = pl.pallas_call(
            stream,
            out_shape=jax.ShapeDtypeStruct((SLOTS * 108, 128), f32),
            in_specs=[smem, vmem, vmem, vmem],
            out_specs=hbm,
            scratch_shapes=[
                pltpu.VMEM((4, 216, 128), f32),
                pltpu.VMEM((SLOTS * 108, 128), f32),
                dma((SLOTS // 2,)),
            ],
        )(places, post, cols, rows)
        return out.reshape(1, 1, SLOTS, 27, 512)

    return jax.shard_map(
        on_device,
        mesh=mesh,
        in_specs=(
            P("curve", "line", None, None, None),
            P("curve", "line", None),
            P(),
            P(None, None, "curve", None),
            P(),
        ),
        out_specs=P("curve", "line", None, None, None),
        check_vma=False,
    )
```

```python
import functools

import jax
import jax.numpy as jnp
import numpy as np
from jax import lax
from jax.experimental import pallas as pl
from jax.experimental.pallas import tpu as pltpu
from jax.sharding import PartitionSpec as P

SLOTS = 6
MESH = pl.DeviceIdType.MESH
TWO_PI = 6.283185307179586
PRODUCT = lax.Precision.HIGH


def along(items, stride, fn):
    done = list(items)
    for base in range(27):
        if (base // stride) % 3 == 0:
            at = (base, base + stride, base + 2 * stride)
            got = fn(*(items[n] for n in at))
            for n, value in zip(at, got):
                done[n] = value
    return done


def to_moments(low, mid, high):
    both = (low + high) * (1.0 / 6.0)
    return both + mid * (2.0 / 3.0), (high - low) * (1.0 / 6.0), both


def from_moments(m0, m1, m2):
    return (m2 - m1) * 3.0, (m0 - m2) * 1.5, (m1 + m2) * 3.0


def dot(a, b, dims=((1,), (0,))):
    return lax.dot_general(a, b, (dims, ((), ())), precision=PRODUCT,
                           preferred_element_type=jnp.float32)


def lroll(x, shift):
    shift = shift % 128
    return x if shift == 0 else pltpu.roll(x, shift, 1)


def sroll(x, shift):
    return pltpu.roll(x, shift % 8, 0)


def collide(nc, nl, keys, waves, rates, x_in, tgt_in, post, cols_ref, rows_ref,
            x_ref, tgt_ref, g, psend, precv, xsend, xmsg, xrecv, ysend, yrecv, yside,
           ps_sem, pr_sem, xs_sem, xr_sem, ys_sem, yr_sem, ds_sem, dr_sem, io_sem):
    ci = lax.axis_index("curve")
    li = lax.axis_index("line")

    fetch = pltpu.make_async_copy(x_in, x_ref, io_sem.at[0])
    fetch.start()
    fetch_target = pltpu.make_async_copy(tgt_in, tgt_ref, io_sem.at[1])
    fetch_target.start()

    def line_at(d):
        return lax.rem(li + (d + nl), nl)

    def curve_at(d):
        return lax.rem(ci + (d + nc), nc)

    barrier = pltpu.get_barrier_semaphore()
    friends = [{"curve": ci, "line": line_at(d)} for d in range(1, nl)]
    friends += [{"curve": curve_at(dy), "line": line_at(dx)} for dy in (-1, 1) for dx in (-1, 0, 1)]
    for friend in friends:
        pl.semaphore_signal(barrier, inc=1, device_id=friend, device_id_type=MESH)

    shape = (8, 128)
    lane = lax.broadcasted_iota(jnp.int32, shape, 1)
    sub = lax.broadcasted_iota(jnp.int32, shape, 0)
    q = lane & 15
    chunk = lane >> 4
    tx = sub & 3
    key = [keys[0, 0, s] for s in range(SLOTS)]

    present = sub == key[0]
    for s in range(1, SLOTS):
        present = jnp.logical_or(present, sub == key[s])
    fluid = jnp.where(present, 1.0, 0.0).astype(jnp.float32)
    solid = 1.0 - fluid

    def wave_lanes(ids):
        m = ids & 7
        out = jnp.full(ids.shape, waves[0], jnp.int32)
        for n in range(1, 8):
            out = jnp.where(m == n, waves[n], out)
        return out

    total_x = nl * 64
    unit = TWO_PI / total_x
    lane16 = lax.broadcasted_iota(jnp.int32, (16, 128), 1)
    row16 = lax.broadcasted_iota(jnp.int32, (16, 128), 0)
    turn = lax.rem(wave_lanes(lane16) * row16, total_x)
    turn = jnp.where((lane16 & 15) >= 8, turn - total_x // 4, turn)
    small = jnp.cos(turn.astype(jnp.float32) * unit)
    rowb = lax.broadcasted_iota(jnp.int32, (128, 128), 0)
    laneb = lax.broadcasted_iota(jnp.int32, (128, 128), 1)
    basis = jnp.where((rowb >> 4) == (laneb >> 4), jnp.concatenate([small] * 8, axis=0), 0.0)

    start = lax.rem(wave_lanes(lane) * ((li * 4 + tx) * 16), total_x)
    angle = start.astype(jnp.float32) * unit
    cos0 = jnp.cos(angle)
    sin0 = jnp.cos((start - total_x // 4).astype(jnp.float32) * unit)
    is_sin = q >= 8
    sin_signed = jnp.where(is_sin, sin0, -sin0)
    cos96 = jnp.concatenate([cos0] * 12, axis=0)
    sin96 = jnp.concatenate([sin_signed] * 12, axis=0)
    is_sin96 = (lax.broadcasted_iota(jnp.int32, (96, 128), 1) & 15) >= 8

    def swapped(t):
        return jnp.where(is_sin96, pltpu.roll(t, 8, 1), pltpu.roll(t, 120, 1))

    r24 = lax.broadcasted_iota(jnp.int32, (24, 96), 0)
    c96 = lax.broadcasted_iota(jnp.int32, (24, 96), 1)
    same = (r24 >> 2) == (c96 >> 4)
    same = jnp.logical_and(same, ((r24 >> 1) & 1) == ((c96 >> 2) & 1))
    same = jnp.logical_and(same, (r24 & 1) == ((c96 >> 3) & 1))
    gather = jnp.where(same, 1.0, 0.0).astype(jnp.float32)

    fetch.wait()
    for p in range(8):
        slot = jnp.int32(0)
        for s in range(SLOTS):
            slot = jnp.where(key[s] == p, s, slot)
        for v in range(4):
            g[v, pl.ds(p, 27, stride=8), :] = x_ref[pl.ds(slot * 108 + v, 27, stride=4), :]

    velocity = [[None] * 4 for _ in range(3)]
    for v in range(4):
        f = [g[v, pl.ds(8 * j, 8), :] for j in range(27)]
        for stride in (1, 3, 9):
            f = along(f, stride, to_moments)
        for j in range(27):
            g[v, pl.ds(8 * j, 8), :] = f[j]
        scale = fluid / f[0]
        for k, j in enumerate((9, 3, 1)):
            velocity[k][v] = f[j] * scale

    stack = jnp.concatenate([velocity[k][v] for k in range(3) for v in range(4)], axis=0)
    local = dot(stack, basis)
    local = local * cos96 + swapped(local) * sin96
    psend[...] = dot(gather, local)

    pl.semaphore_wait(barrier, len(friends))

    copies = []
    for d in range(1, nl):
        copy = pltpu.make_async_remote_copy(
            src_ref=psend, dst_ref=precv.at[d - 1], send_sem=ps_sem.at[d - 1],
            recv_sem=pr_sem.at[d - 1], device_id={"curve": ci, "line": line_at(d)},
            device_id_type=MESH)
        copy.start()
        copies.append(copy)
    fetch_target.wait()
    ry = lax.broadcasted_iota(jnp.int32, (32, 512), 0)
    ly = lax.broadcasted_iota(jnp.int32, (32, 512), 1)
    spread = dot(tgt_ref[...], jnp.where((ly >> 4) == ry, 1.0, 0.0).astype(jnp.float32))
    rm = lax.broadcasted_iota(jnp.int32, (96, 512), 0)
    lm = lax.broadcasted_iota(jnp.int32, (96, 512), 1)
    spread = jnp.where((rm & 15) == (lm & 15), spread, 0.0)
    target = jnp.zeros((24, 128), jnp.float32)
    for yy in range(4):
        pick = jnp.logical_and((r24 >> 2) == (c96 >> 4), (r24 & 3) == yy)
        target = target + dot(jnp.where(pick, 1.0, 0.0).astype(jnp.float32),
                              spread[:, 128 * yy:128 * yy + 128])

    total = psend[...]
    for d in range(1, nl):
        copies[d - 1].wait_recv()
        total = total + precv[d - 1]

    misfit = 0.5 * (target - (2.0 / total_x) * total)
    wide = dot(gather, misfit, ((0,), (0,)))
    wide = wide * cos96 - swapped(wide) * sin96
    nudge = dot(wide, basis, ((1,), (1,)))

    for v in range(4):
        m = [g[v, pl.ds(8 * j, 8), :] for j in range(27)]
        powers = []
        for k in range(3):
            at = 8 * (4 * k + v)
            shifted = velocity[k][v] + nudge[at:at + 8, :]
            powers.append((None, shifted, shifted * shifted + 1.0 / 3.0))
        relaxed = []
        for a in range(3):
            along_a = m[0] if a == 0 else m[0] * powers[0][a]
            for b in range(3):
                along_b = along_a if b == 0 else along_a * powers[1][b]
                for c in range(3):
                    eq = along_b if c == 0 else along_b * powers[2][c]
                    j = 9 * a + 3 * b + c
                    relaxed.append(m[j] - rates[j] * (m[j] - eq))
        for stride in (1, 3, 9):
            relaxed = along(relaxed, stride, from_moments)
        for j in range(27):
            post[v, pl.ds(8 * j, 8), :] = relaxed[j]

    def at(j, v):
        return post[v, pl.ds(8 * j, 8), :]

    halo = []
    for n, cy in enumerate((1, -1)):
        for cx in (-1, 0, 1):
            pack = solid
            for cz in range(3):
                for z in range(2):
                    c = 2 * cz + z
                    j = 9 * (cx + 1) + 3 * (cy + 1) + cz
                    if cy == 1:
                        moved = lroll(at(j, 2 * z + 1), 16 * c - 112)
                    else:
                        moved = lroll(at(j, 2 * z), 16 * c)
                    pack = jnp.where(chunk == c, moved, pack)
            ysend[n, cx + 1] = pack
        for e, cx in enumerate((1, -1)):
            halo.append(pltpu.make_async_remote_copy(
                src_ref=ysend.at[n, cx + 1], dst_ref=yside.at[n, e],
                send_sem=ds_sem.at[n, e], recv_sem=dr_sem.at[n, e],
                device_id={"curve": curve_at(cy), "line": line_at(cx)},
                device_id_type=MESH))
            halo[-1].start()
        halo.append(pltpu.make_async_remote_copy(
            src_ref=ysend.at[n], dst_ref=yrecv.at[n], send_sem=ys_sem.at[n],
            recv_sem=yr_sem.at[n], device_id={"curve": curve_at(cy), "line": li},
            device_id_type=MESH))
        halo[-1].start()
    for n, cx in enumerate((1, -1)):
        merged = jnp.zeros(shape, jnp.float32)
        for v in range(4):
            pack = solid
            for k in range(9):
                moved = lroll(at(9 * (cx + 1) + k, v), k - 15 if cx == 1 else k)
                pack = jnp.where(q == k, moved, pack)
            xsend[n, v] = pack
            merged = jnp.where(tx == v, sroll(pack, v - 3 if cx == 1 else v), merged)
        xmsg[n] = merged
        halo.append(pltpu.make_async_remote_copy(
            src_ref=xmsg.at[n], dst_ref=xrecv.at[n], send_sem=xs_sem.at[n],
            recv_sem=xr_sem.at[n], device_id={"curve": ci, "line": line_at(cx)},
            device_id_type=MESH))
        halo[-1].start()
    for copy in halo:
        copy.wait_recv()

    def beside(own, other, cx):
        if cx == 1:
            return jnp.where(tx == 0, sroll(other, 5), sroll(own, 1))
        return jnp.where(tx == 3, sroll(other, 3), sroll(own, 7))

    def x_edge(cx):
        return q == (0 if cx == 1 else 15)

    for n, cy in enumerate((1, -1)):
        for cx in (-1, 0, 1):
            row = yrecv[n, cx + 1]
            if cx != 0:
                near = beside(row, yside[n, 0 if cx == 1 else 1], cx)
                row = jnp.where(x_edge(cx), lroll(near, -15 * cx), lroll(row, cx))
            rows_ref[n, cx + 1] = sroll(row, 4)
    for n, cx in enumerate((1, -1)):
        for v in range(4):
            own, other = xsend[n, v], xrecv[n]
            if cx == 1:
                cols_ref[n, v] = jnp.where(tx == 0, sroll(other, -v), sroll(own, 1))
            else:
                cols_ref[n, v] = jnp.where(tx == 3, sroll(other, 3 - v), sroll(own, 7))
    for copy in copies + halo:
        copy.wait_send()


def stream(keys, post, cols_ref, rows_ref, out, g, out_ref, sem):
    shape = (8, 128)
    lane = lax.broadcasted_iota(jnp.int32, shape, 1)
    sub = lax.broadcasted_iota(jnp.int32, shape, 0)
    q = lane & 15
    key = [keys[0, 0, s] for s in range(SLOTS)]

    present = sub == key[0]
    for s in range(1, SLOTS):
        present = jnp.logical_or(present, sub == key[s])
    solid = jnp.where(present, 0.0, 1.0).astype(jnp.float32)

    def at(j, v):
        return post[v, pl.ds(8 * j, 8), :]

    def x_edge(cx):
        return q == (0 if cx == 1 else 15)

    def step_x(own, cx, k, v):
        if cx == 0:
            return own
        near = lroll(cols_ref[0 if cx == 1 else 1, v], -k if cx == 1 else 15 - k)
        return jnp.where(x_edge(cx), near, lroll(own, cx))

    def step_y(a0, a1, cx, cy, c):
        if cy == 0:
            return a0, a1
        r0, r1 = lroll(a0, 16 * cy), lroll(a1, 16 * cy)
        if cy == 1:
            row = lroll(rows_ref[0 if cy == 1 else 1, cx + 1], -16 * c)
            row = jnp.where(sub < 4, row, sroll(r1, 4))
            return jnp.where(lane < 16, row, r0), jnp.where(lane < 16, r0, r1)
        row = lroll(rows_ref[0 if cy == 1 else 1, cx + 1], 112 - 16 * c)
        row = jnp.where(sub >= 4, row, sroll(r0, 4))
        return jnp.where(lane >= 112, r1, r0), jnp.where(lane >= 112, row, r1)

    for cx in (-1, 0, 1):
        for cy in (-1, 0, 1):
            base = 9 * (cx + 1) + 3 * (cy + 1)
            if cx == 0 and cy == 0:
                blocked = None
            else:
                wall = step_x(solid, cx, 9, 0)
                walls = step_y(wall, wall, cx, cy, 6)
                blocked = [w > 0.5 for w in walls]

            def moved(cz, z):
                j = base + cz
                k = 3 * (cy + 1) + cz
                a = [step_x(at(j, 2 * z + h), cx, k, 2 * z + h) for h in range(2)]
                return step_y(a[0], a[1], cx, cy, 2 * cz + z)

            def put(cz, z, source):
                j = base + cz
                for h in range(2):
                    value = at(26 - j, 2 * z + h)
                    if source is not None:
                        value = source[h] if blocked is None else jnp.where(blocked[h], value, source[h])
                    g[2 * z + h, pl.ds(8 * j, 8), :] = value

            put(1, 0, moved(1, 0))
            put(1, 1, moved(1, 1))
            put(2, 0, None)
            put(2, 1, moved(2, 0))
            put(0, 0, moved(0, 1))
            put(0, 1, moved(2, 1))

    writes = []
    for s in range(SLOTS):
        place = jnp.maximum(key[s], 0)
        keep = jnp.where(key[s] >= 0, 1.0, 0.0).astype(jnp.float32)
        for v in range(4):
            out_ref[pl.ds(108 * s + v, 27, stride=4), :] = g[v, pl.ds(place, 27, stride=8), :] * keep
        if s % 2 == 1:
            part = pl.ds(108 * (s - 1), 216)
            writes.append(pltpu.make_async_copy(out_ref.at[part], out.at[part], sem.at[s // 2]))
            writes[-1].start()
    for copy in writes:
        copy.wait()


def solution(mesh):
    nc, nl = mesh.shape["curve"], mesh.shape["line"]

    def on_device(scaled, places, waves, amplitudes, rates):
        x = scaled.reshape(SLOTS * 108, 128)
        target = amplitudes.transpose(0, 1, 3, 2).reshape(96, 32)
        vmem = pl.BlockSpec(memory_space=pltpu.VMEM)
        hbm = pl.BlockSpec(memory_space=pl.ANY)
        smem = pl.BlockSpec(memory_space=pltpu.SMEM)
        f32 = jnp.float32
        dma = pltpu.SemaphoreType.DMA
        post, cols, rows = pl.pallas_call(
            functools.partial(collide, nc, nl),
            out_shape=[
                pltpu.VMEM((4, 216, 128), f32),
                pltpu.VMEM((2, 4, 8, 128), f32),
                pltpu.VMEM((2, 3, 8, 128), f32),
            ],
            in_specs=[smem, smem, smem, hbm, hbm],
            out_specs=[vmem] * 3,
            scratch_shapes=[
                pltpu.VMEM((SLOTS * 108, 128), f32),
                pltpu.VMEM((96, 32), f32),
                pltpu.VMEM((4, 216, 128), f32),
                pltpu.VMEM((24, 128), f32),
                pltpu.VMEM((nl - 1, 24, 128), f32),
                pltpu.VMEM((2, 4, 8, 128), f32),
                pltpu.VMEM((2, 8, 128), f32),
                pltpu.VMEM((2, 8, 128), f32),
                pltpu.VMEM((2, 3, 8, 128), f32),
                pltpu.VMEM((2, 3, 8, 128), f32),
                pltpu.VMEM((2, 2, 8, 128), f32),
                dma((nl - 1,)), dma((nl - 1,)),
                dma((2,)), dma((2,)), dma((2,)), dma((2,)),
                dma((2, 2)), dma((2, 2)), dma((2,)),
            ],
            compiler_params=pltpu.CompilerParams(collective_id=0, has_side_effects=True),
        )(places, waves, rates, x, target)
        post, cols, rows = (
            pltpu.with_memory_space_constraint(a, pltpu.VMEM) for a in (post, cols, rows))
        out = pl.pallas_call(
            stream,
            out_shape=jax.ShapeDtypeStruct((SLOTS * 108, 128), f32),
            in_specs=[smem, vmem, vmem, vmem],
            out_specs=hbm,
            scratch_shapes=[
                pltpu.VMEM((4, 216, 128), f32),
                pltpu.VMEM((SLOTS * 108, 128), f32),
                dma((SLOTS // 2,)),
            ],
        )(places, post, cols, rows)
        return out.reshape(1, 1, SLOTS, 27, 512)

    return jax.shard_map(
        on_device,
        mesh=mesh,
        in_specs=(
            P("curve", "line", None, None, None),
            P("curve", "line", None),
            P(),
            P(None, None, "curve", None),
            P(),
        ),
        out_specs=P("curve", "line", None, None, None),
        check_vma=False,
    )
```
